32 devices in a mesh: dp: 8 (over z, core), expert: 4 (over y, x).
Axes of the slice: x: 2, y: 2, z: 4, core: 2. Of those that a mesh axis runs over, the one named last changes fastest.
Arguments:
- cached_hidden: bfloat16 [1024, 1536], P(('dp', 'expert')), may hold values from -6 to 6
- direction: bfloat16 [4, 2880, 1536], P('expert', 'dp'), may hold values from -1 to 1
- expert_ids: int32 [4096, 4], P(('dp', 'expert')), may hold values from 0 to 127, as said below
- gate_weights: float32 [4096, 4], P(('dp', 'expert')), may hold values from 0.05 to 1
Outputs:
- curvature_product: float32 [4, 2880, 1536], P('expert', 'dp')
The draws below stay inside these ranges and needn't reach their ends.
Inputs may be any that keep to these rules, and one draw needn't show every extreme that they name: `expert_ids`: each row names 4 different experts, at most two of them below 4. Among the 128 rows of one device no expert below 4 is named more than 8 times; for every dp index, some expert below 4 is named exactly 8 times by the rows of each device with that dp index.
All inputs are finite; a program needn't handle non-finite values.
Results may differ from the reference program's by a relative error of at most 0.0034.
Values may be sent and summed in bfloat16 or wider, within the bound.
A program may use at most 128 MiB of HBM per device.

```python
import math
import jax
import jax.numpy as jnp
from jax import lax

D = 2880
FW = 1536
ALL_EXPERTS = 128
TOPK = 4
T_DEV = 128
EXPERTS = 4
CAP = 8
TOKENS = 4096
N_DP = 8
N_EXPERT = 4


def draw_expert_ids(key, part):
    out_band = (ALL_EXPERTS - EXPERTS) // TOPK

    def one_block(position):
        row_number = position // N_EXPERT
        block_key = jax.random.fold_in(key, position)
        row_key = jax.random.fold_in(key, 7919 * N_DP * N_EXPERT + row_number)
        sub_keys = jax.random.split(block_key, 4)
        full_one = jax.random.randint(row_key, (), 0, EXPERTS)
        counts = jax.random.randint(sub_keys[0], (EXPERTS,), CAP // 4, CAP // 2 + 1)
        counts = jnp.where(jnp.arange(EXPERTS) == full_one, CAP, counts).astype(jnp.int32)
        bounds = jnp.cumsum(counts)
        filled = bounds[-1]
        half_point = jnp.maximum((filled + 1) // 2, CAP)
        order = jax.random.permutation(sub_keys[1], T_DEV).astype(jnp.int32)
        rotate = jax.random.randint(sub_keys[2], (T_DEV,), 0, TOPK)
        outside = EXPERTS + jnp.arange(TOPK)[None, :] * out_band + jax.random.randint(sub_keys[3], (T_DEV, TOPK), 0, out_band)
        columns = []
        for choice_rank in range(TOPK):
            column = (choice_rank - rotate) % TOPK
            pair = order + column * half_point
            limit = jnp.where(column == 0, half_point, filled)
            inner = jnp.sum((bounds[None, :] <= pair[:, None]).astype(jnp.int32), axis=1)
            usable = (column < 2) & (pair < limit)
            columns.append(jnp.where(usable, inner, outside[:, choice_rank]))
        return jnp.stack(columns, axis=1).astype(jnp.int32)
    blocks = jax.vmap(one_block)(jnp.arange(N_DP * N_EXPERT, dtype=jnp.int32))
    return blocks.reshape(N_DP * N_EXPERT * T_DEV, TOPK).astype(jnp.int32)


def block_positions(block_ids):
    flat = block_ids.reshape(-1)
    onehot = (flat[:, None] == jnp.arange(EXPERTS, dtype=jnp.int32)[None, :]).astype(jnp.int32)
    before = jnp.cumsum(onehot, axis=0) - onehot
    return jnp.sum(before * onehot, axis=1).astype(jnp.int32).reshape(block_ids.shape)


def slot_tokens(key, part):
    ids_four = draw_expert_ids(key, part).reshape(N_DP, N_EXPERT, T_DEV, TOPK)
    slot_pos = jax.vmap(jax.vmap(block_positions))(ids_four)
    treated = ids_four < EXPERTS
    owner_index = jnp.where(treated, ids_four, EXPERTS).astype(jnp.int32)
    row_index = jnp.broadcast_to(jnp.arange(N_DP, dtype=jnp.int32)[:, None, None, None], ids_four.shape)
    source_index = jnp.broadcast_to(jnp.arange(N_EXPERT, dtype=jnp.int32)[None, :, None, None], ids_four.shape)
    local_index = jnp.broadcast_to(jnp.arange(T_DEV, dtype=jnp.int32)[None, None, :, None], ids_four.shape)
    token_index = ((row_index * N_EXPERT + source_index) * T_DEV + local_index).astype(jnp.int32)
    table = jnp.full((N_DP, EXPERTS, N_EXPERT, CAP), -1, jnp.int32)
    table = table.at[row_index, owner_index, source_index, slot_pos].set(token_index, mode='drop')
    spare = TOKENS + jnp.arange(N_DP * EXPERTS * N_EXPERT * CAP, dtype=jnp.int32).reshape(table.shape)
    return jnp.where(table >= 0, table, spare).astype(jnp.int32)


def draw_cached_hidden(key, part):
    token_table = slot_tokens(key, part).reshape(N_DP, EXPERTS * N_EXPERT * CAP)
    shared_key = jax.random.fold_in(key, 1000003)
    noise_key = jax.random.fold_in(key, 1000033)

    def shared_row(token):
        row_key = jax.random.fold_in(shared_key, token)
        return jax.random.normal(row_key, (FW,), jnp.float32)

    def one_row_block(inputs):
        row_number, token_list = inputs
        shared = jax.vmap(shared_row)(token_list)
        block_key = jax.random.fold_in(noise_key, row_number)
        noise = jax.random.normal(block_key, (token_list.shape[0], FW), jnp.float32)
        rows = 0.9 * shared + 0.436 * noise
        return jnp.clip(rows, -6.0, 6.0).astype(jnp.bfloat16)
    blocks = lax.map(one_row_block, (jnp.arange(N_DP, dtype=jnp.int32), token_table))
    return blocks.reshape(N_DP * EXPERTS * N_EXPERT * CAP, FW)


def draw_direction(key, part):
    common_key = jax.random.fold_in(key, 2000003)
    own_key = jax.random.fold_in(key, 2000029)
    common = jax.random.normal(common_key, (D, FW), jnp.float32)
    own = jax.random.normal(own_key, (EXPERTS, D, FW), jnp.float32)
    mixed = (0.8 * common[None, :, :] + 0.6 * own) * (1.0 / math.sqrt(FW))
    limit = min(1.0, 6.0 / math.sqrt(FW))
    return jnp.clip(mixed, -limit, limit).astype(jnp.bfloat16)


def block_levels(stream_key, dims, shards, least, largest):
    factor_of = 1.0
    for dim, blocks in shards:
        steps = jax.random.uniform(jax.random.fold_in(jax.random.fold_in(stream_key, 6), dim), (blocks,), jnp.float32, least / len(shards), largest / len(shards))
        factor_of = factor_of * jnp.repeat(jnp.exp(steps), dims[dim] // blocks).reshape((-1,) + (1,) * (len(dims) - 1 - dim))
    return factor_of


def setup_inputs(seed: int = 0) -> dict:
    key_of = jax.random.split(jax.random.key(seed), 5)
    return {
        "cached_hidden": draw_cached_hidden(jax.random.fold_in(key_of[4], 71), 0),
        "direction": draw_direction(jax.random.fold_in(key_of[4], 71), 0),
        "expert_ids": draw_expert_ids(jax.random.fold_in(key_of[4], 71), 0),
        "gate_weights": jnp.clip(jnp.exp(math.log(1.0) - 2.9957323 * jax.random.uniform(key_of[3], (TOKENS, TOPK), jnp.float32) ** block_levels(key_of[3], (TOKENS, TOPK), ((0, 32),), -0.2, 0.2)), 0.05, 1.0),
    }


def slot_positions(block_ids, experts):
    flat = block_ids.reshape(-1)
    onehot = (flat[:, None] == jnp.arange(experts, dtype=jnp.int32)[None, :]).astype(jnp.int32)
    before = jnp.cumsum(onehot, axis=0) - onehot
    return lax.optimization_barrier(jnp.sum(before * onehot, axis=1)).astype(jnp.int32).reshape(block_ids.shape)

def reference(cached_hidden, direction, expert_ids, gate_weights):
    rows_five = cached_hidden.reshape(N_DP, EXPERTS, N_EXPERT, CAP, FW)

    def forward(owner):
        block = rows_five[:, owner].reshape(-1, FW)
        result = lax.dot_general(block, direction[owner], (((1,), (1,)), ((), ())), preferred_element_type=jnp.float32)
        return result.astype(jnp.bfloat16).reshape(N_DP, N_EXPERT, CAP, D)
    tangent = lax.map(forward, jnp.arange(EXPERTS, dtype=jnp.int32))
    ids_four = expert_ids.reshape(N_DP, N_EXPERT, T_DEV, TOPK)
    treated = ids_four < EXPERTS
    safe_ids = jnp.where(treated, ids_four, 0).astype(jnp.int32)
    drop_ids = jnp.where(treated, ids_four, EXPERTS).astype(jnp.int32)
    slot_pos = jax.vmap(jax.vmap(lambda blk: slot_positions(blk, EXPERTS)))(ids_four)
    row_index = jnp.broadcast_to(jnp.arange(N_DP, dtype=jnp.int32)[:, None, None, None], ids_four.shape)
    source_index = jnp.broadcast_to(jnp.arange(N_EXPERT, dtype=jnp.int32)[None, :, None, None], ids_four.shape)
    picked = tangent[safe_ids, row_index, source_index, slot_pos]
    gates_four = jnp.where(treated, gate_weights.reshape(N_DP, N_EXPERT, T_DEV, TOPK), 0.0)
    scale_factor = 1.0 / math.sqrt(TOKENS)
    combined = lax.optimization_barrier(jnp.sum(gates_four[..., None] * picked.astype(jnp.float32), axis=3)) * scale_factor
    outgoing = (gates_four[..., None] * combined[:, :, :, None, :]).astype(jnp.bfloat16)
    adjoint = jnp.zeros((EXPERTS, N_DP, N_EXPERT, CAP, D), jnp.bfloat16)
    adjoint = adjoint.at[drop_ids, row_index, source_index, slot_pos].set(outgoing, mode='drop')

    def backward(owner):
        block = rows_five[:, owner].reshape(-1, FW)
        adj_rows = adjoint[owner].reshape(-1, D)
        return lax.dot_general(adj_rows, block, (((0,), (0,)), ((), ())), preferred_element_type=jnp.float32)
    return lax.map(backward, jnp.arange(EXPERTS, dtype=jnp.int32))
```

```python
import functools
import math

import jax
import jax.numpy as jnp
from jax import lax
from jax.experimental import pallas as pl
from jax.experimental.pallas import tpu as pltpu
from jax.sharding import PartitionSpec as P

MESH = pl.DeviceIdType.MESH
CORES = 2
LANES = 128
CHUNKS = 2


def slot_positions(block_ids, experts):
    flat = block_ids.reshape(-1)
    onehot = (flat[:, None] == jnp.arange(experts, dtype=jnp.int32)[None, :]).astype(jnp.int32)
    before = jnp.cumsum(onehot, axis=0) - onehot
    return jnp.sum(before * onehot, axis=1).reshape(block_ids.shape)


def general_body(cached_hidden, direction, expert_ids, gate_weights):
    dp_count = lax.axis_size("dp")
    owner_count = lax.axis_size("expert")
    slot_rows = cached_hidden.shape[0]
    capacity = slot_rows // owner_count
    tok_count = expert_ids.shape[0]
    width = direction.shape[1] * dp_count
    local_dir = direction[0]
    rows_all = lax.all_gather(cached_hidden, "dp", axis=0, tiled=True)
    tangent = lax.dot_general(
        rows_all, local_dir, (((1,), (1,)), ((), ())), preferred_element_type=jnp.float32
    )
    tangent = tangent.astype(jnp.bfloat16).reshape(
        dp_count, owner_count, capacity, local_dir.shape[0]
    )
    returned = lax.all_to_all(
        lax.all_to_all(tangent, "dp", split_axis=0, concat_axis=3, tiled=True),
        "expert",
        split_axis=1,
        concat_axis=1,
        tiled=True,
    )
    flat_rows = returned.reshape(owner_count * capacity, width)
    treated = expert_ids < owner_count
    slot_pos = slot_positions(expert_ids, owner_count)
    target = expert_ids * capacity + slot_pos
    lookup = jnp.where(treated, target, 0).reshape(-1)
    dropped = jnp.where(treated, target, owner_count * capacity).reshape(-1)
    gates = jnp.where(treated, gate_weights, 0.0)
    picked = jnp.take(flat_rows, lookup, axis=0).reshape(tok_count, expert_ids.shape[1], width)
    scale_factor = 1.0 / math.sqrt(tok_count * dp_count * owner_count)
    combined = jnp.sum(gates[..., None] * picked.astype(jnp.float32), axis=1) * scale_factor
    outgoing = (gates[..., None] * combined[:, None, :]).astype(jnp.bfloat16)
    buffer = jnp.zeros((owner_count * capacity, width), jnp.bfloat16)
    buffer = buffer.at[dropped].set(outgoing.reshape(-1, width), mode="drop")
    buffer = buffer.reshape(1, owner_count, capacity, width)
    arrived = lax.all_to_all(buffer, "expert", split_axis=1, concat_axis=1, tiled=True)
    adjoint = lax.all_to_all(arrived, "dp", split_axis=3, concat_axis=0, tiled=True)
    adjoint_rows = adjoint.reshape(-1, adjoint.shape[3])
    gradient = lax.dot_general(
        adjoint_rows, rows_all, (((0,), (0,)), ((), ())), preferred_element_type=jnp.float32
    )
    return gradient.reshape(1, gradient.shape[0], gradient.shape[1])


def swap_blocks(x, cap):
    lane = lax.broadcasted_iota(jnp.int32, x.shape, 1)
    back = pltpu.roll(x, LANES - cap, 1)
    ahead = pltpu.roll(x, cap, 1)
    return jnp.where((lane // cap) % 2 == 0, back, ahead)


def pair_matrix(ids, gates, q, n_e, cap, scale):
    toks, topk = ids.shape
    lane = lax.broadcasted_iota(jnp.int32, (toks, LANES), 1)
    lane_e, lane_q, lane_c = lane // (n_e * cap), (lane // cap) % n_e, lane % cap
    named = jnp.zeros((toks, LANES), jnp.float32)
    gate = jnp.zeros((toks, LANES), jnp.float32)
    for k in range(topk):
        same = ids[:, k : k + 1] == lane_e
        named = named + jnp.where(same, 1.0, 0.0)
        gate = gate + jnp.where(same, gates[:, k : k + 1], 0.0)
    row = lax.broadcasted_iota(jnp.int32, (toks, toks), 0)
    col = lax.broadcasted_iota(jnp.int32, (toks, toks), 1)
    earlier = jnp.where(col < row, 1.0, 0.0).astype(jnp.bfloat16)
    position = jnp.dot(earlier, named.astype(jnp.bfloat16), preferred_element_type=jnp.float32)
    held = (position == lane_c.astype(jnp.float32)) & (lane_q == q)
    slots = jnp.where(held, gate, 0.0).T
    high = slots.astype(jnp.bfloat16)
    low = (slots - high.astype(jnp.float32)).astype(jnp.bfloat16)
    nt = (((1,), (1,)), ((), ()))
    total = lax.dot_general(high, high, nt, preferred_element_type=jnp.float32)
    total += lax.dot_general(high, low, nt, preferred_element_type=jnp.float32)
    total += lax.dot_general(low, high, nt, preferred_element_type=jnp.float32)
    return total * scale


def kernel(
    n_dp, n_e, cap, scale,
    h_ref, dir_ref, ids_ref, gates_ref,
    adj_ref, hall,
    dirv, tang, pairs, wf, wall,
    loc_sem, own_send, relay_send, hz_recv, hs_send, hs_recv,
    a_send, a_recv, w_send, w_recv, ws_send, ws_recv, t_send, t_recv,
):
    n_z = n_dp // CORES
    rows = n_e * cap
    feat = dirv.shape[0]
    part = rows // CHUNKS
    p = lax.axis_index("dp")
    e = lax.axis_index("expert")
    z, core = p // CORES, p % CORES
    sib = z * CORES + (1 - core)
    nt = (((1,), (1,)), ((), ()))

    load_dir = pltpu.make_async_copy(dir_ref.at[0], dirv, loc_sem.at[0])
    load_h = pltpu.make_async_copy(h_ref, hall.at[p], loc_sem.at[1])
    load_dir.start()
    load_h.start()

    def z_peer(d):
        return lax.rem(z + d, n_z)

    def e_peer(d):
        return lax.rem(e + d, n_e)

    barrier = pltpu.get_barrier_semaphore()
    for d in range(1, n_z):
        pl.semaphore_signal(barrier, inc=1, device_id=(z_peer(d) * CORES + core, e), device_id_type=MESH)
    for d in range(1, n_e):
        pl.semaphore_signal(barrier, inc=1, device_id=(p, e_peer(d)), device_id_type=MESH)
    pl.semaphore_signal(barrier, inc=1, device_id=(sib, e), device_id_type=MESH)
    pl.semaphore_wait(barrier, n_z + n_e - 1)

    def remote(src, dst, send, recv, dev):
        return pltpu.make_async_remote_copy(
            src_ref=src, dst_ref=dst, send_sem=send, recv_sem=recv, device_id=dev, device_id_type=MESH
        )

    def own_copy(side, c):
        to = z + 1 if side == 0 else z - 1
        return remote(
            h_ref.at[pl.ds(c * part, part)], hall.at[p, pl.ds(c * part, part)],
            own_send.at[side, c], hz_recv.at[z, c], (to * CORES + core, e),
        )

    def on_side(side, fn):
        pl.when(z + 1 < n_z if side == 0 else z > 0)(fn)

    for c in range(CHUNKS):
        for side in range(2):
            on_side(side, lambda side=side, c=c: own_copy(side, c).start())

    def sibling_copy(zs, src):
        row = zs * CORES + core
        return remote(src, hall.at[row], hs_send.at[zs], hs_recv.at[zs], (sib, e))

    sibling_copy(z, h_ref).start()

    pairs[...] = pair_matrix(ids_ref[...], gates_ref[...], e, n_e, cap, scale)

    def slot_rows(owner, source):
        return pl.ds(pl.multiple_of(owner * rows + source * cap, cap), cap)

    def pair_copy(d):
        to = e_peer(d)
        return remote(
            pairs.at[slot_rows(to, e)], wf.at[pl.ds(pl.multiple_of(e * cap, cap), cap)],
            a_send.at[d], a_recv.at[e], (p, to),
        )

    for d in range(1, n_e):
        pair_copy(d).start()
    wf[pl.ds(pl.multiple_of(e * cap, cap), cap), :] = pairs[slot_rows(e, e), :]

    mine = pl.ds(pl.multiple_of(e * rows, rows), rows)
    tang[:, mine, feat // LANES * LANES :] = jnp.zeros(
        (n_dp, rows, tang.shape[2] - feat // LANES * LANES), jnp.bfloat16
    )

    def tangent_copy(zs, d):
        ref = tang.at[pl.ds(zs * CORES, CORES), mine]
        return remote(ref, ref, t_send.at[zs, d], t_recv.at[zs, e], (p, e_peer(d)))

    def tangents(zs):
        block = hall[pl.ds(zs * CORES, CORES)].reshape(CORES * rows, hall.shape[2])
        out = lax.dot_general(block, dirv[...], nt, preferred_element_type=jnp.float32)
        tang[pl.ds(zs * CORES, CORES), mine, :feat] = out.astype(jnp.bfloat16).reshape(CORES, rows, feat)
        for d in range(1, n_e):
            tangent_copy(zs, d).start()

    load_dir.wait()
    load_h.wait()
    sibling_copy(z, h_ref).wait_recv()
    tangents(z)

    for d in range(1, n_e):
        src = e_peer(d)
        remote(
            pairs.at[slot_rows(e, src)], wf.at[pl.ds(pl.multiple_of(src * cap, cap), cap)],
            a_send.at[d], a_recv.at[src], (p, src),
        ).wait_recv()
    weights = wf[...]
    high = weights.astype(jnp.bfloat16).astype(jnp.float32)
    wall[p] = (high + swap_blocks(weights - high, cap)).astype(jnp.bfloat16)

    def weight_copy(d):
        return remote(wall.at[p], wall.at[p], w_send.at[d], w_recv.at[z], (z_peer(d) * CORES + core, e))

    def weight_sibling(zs):
        ref = wall.at[zs * CORES + core]
        return remote(ref, ref, ws_send.at[zs], ws_recv.at[zs], (sib, e))

    for d in range(1, n_z):
        weight_copy(d).start()
    weight_sibling(z).start()

    near = jnp.minimum(z, n_z - 1 - z)

    def source(j):
        if j == 0:
            return z
        s = (j + 1) // 2
        close = z - s if j % 2 else z + s
        far = jnp.where(2 * z < n_z - 1, j, n_z - 1 - j)
        return jnp.where(j <= 2 * near, close, far)

    def relay_copy(zs, c):
        to = jnp.where(zs < z, z + 1, z - 1)
        ref = hall.at[zs * CORES + core, pl.ds(c * part, part)]
        return remote(ref, ref, relay_send.at[zs, c], hz_recv.at[zs, c], (to * CORES + core, e))

    def relays(zs, fn):
        to = jnp.where(zs < z, z + 1, z - 1)
        pl.when((to >= 0) & (to < n_z))(fn)

    lane = lax.broadcasted_iota(jnp.int32, (rows, LANES), 1)
    row = lax.broadcasted_iota(jnp.int32, (rows, LANES), 0)
    direct = (lane // cap) % n_e == row // cap

    def finish(zs):
        weight_sibling(zs).wait_recv()
        for d in range(1, n_e):
            src = e_peer(d)
            ref = tang.at[pl.ds(zs * CORES, CORES), pl.ds(pl.multiple_of(src * rows, rows), rows)]
            remote(ref, ref, t_send.at[zs, d], t_recv.at[zs, src], (p, src)).wait_recv()
        for k in range(CORES):
            packed = wall[zs * CORES + k].astype(jnp.float32)
            high = jnp.where(direct, packed, 0.0)
            low = swap_blocks(packed - high, cap)
            both = jnp.concatenate([high, low], axis=0).astype(jnp.bfloat16)
            out = jnp.dot(both, tang[zs * CORES + k], preferred_element_type=jnp.float32)
            out = (out[:rows] + out[rows:]).astype(jnp.bfloat16)
            adj_ref[zs * CORES + k] = out[:, :feat]

    for j in range(1, n_z):
        zs = source(j)
        for c in range(CHUNKS):
            relay_copy(zs, c).wait_recv()
            relays(zs, lambda zs=zs, c=c: relay_copy(zs, c).start())
        sibling_copy(zs, hall.at[zs * CORES + core]).start()
        sibling_copy(zs, hall.at[zs * CORES + core]).wait_recv()
        tangents(zs)
        remote(
            wall.at[zs * CORES + core], wall.at[zs * CORES + core], w_send.at[1], w_recv.at[zs], (sib, e)
        ).wait_recv()
        weight_sibling(zs).start()
        finish(source(j - 1))
    finish(source(n_z - 1))

    for c in range(CHUNKS):
        for side in range(2):
            on_side(side, lambda side=side, c=c: own_copy(side, c).wait_send())
    for d in range(1, n_e):
        pair_copy(d).wait_send()
    for d in range(1, n_z):
        weight_copy(d).wait_send()
    for j in range(n_z):
        zs = source(j)
        sibling_copy(zs, hall.at[zs * CORES + core]).wait_send()
        weight_sibling(zs).wait_send()
        for d in range(1, n_e):
            tangent_copy(zs, d).wait_send()
        if j:
            for c in range(CHUNKS):
                relays(zs, lambda zs=zs, c=c: relay_copy(zs, c).wait_send())


def body(cached_hidden, direction, expert_ids, gate_weights):
    n_dp, n_e = lax.axis_size("dp"), lax.axis_size("expert")
    rows, fw = cached_hidden.shape
    cap = rows // n_e
    feat = direction.shape[1]
    if n_e * rows != LANES or cap % 8 or rows % (16 * CHUNKS) or n_dp % CORES or n_dp < 2 * CORES:
        return general_body(cached_hidden, direction, expert_ids, gate_weights)
    n_z = n_dp // CORES
    wide = -(-feat // LANES) * LANES
    scale = 1.0 / math.sqrt(expert_ids.shape[0] * n_dp * n_e)
    vmem = pl.BlockSpec(memory_space=pltpu.VMEM)
    hbm = pl.BlockSpec(memory_space=pl.ANY)
    dma = pltpu.SemaphoreType.DMA
    adjoint, rows_all = pl.pallas_call(
        functools.partial(kernel, n_dp, n_e, cap, scale),
        out_shape=(
            jax.ShapeDtypeStruct((n_dp, rows, feat), jnp.bfloat16),
            jax.ShapeDtypeStruct((n_dp, rows, fw), jnp.bfloat16),
        ),
        in_specs=[hbm, hbm, vmem, vmem],
        out_specs=(vmem, vmem),
        scratch_shapes=[
            pltpu.VMEM((feat, fw), jnp.bfloat16),
            pltpu.VMEM((n_dp, n_e * rows, wide), jnp.bfloat16),
            pltpu.VMEM((LANES, LANES), jnp.float32),
            pltpu.VMEM((rows, LANES), jnp.float32),
            pltpu.VMEM((n_dp, rows, LANES), jnp.bfloat16),
            dma((2,)),
            dma((2, CHUNKS)),
            dma((n_z, CHUNKS)),
            dma((n_z, CHUNKS)),
            dma((n_z,)),
            dma((n_z,)),
            dma((n_e,)),
            dma((n_e,)),
            dma((n_z,)),
            dma((n_z,)),
            dma((n_z,)),
            dma((n_z,)),
            dma((n_z, n_e)),
            dma((n_z, n_e)),
        ],
        compiler_params=pltpu.CompilerParams(
            collective_id=0, has_side_effects=True, vmem_limit_bytes=32 * 1024 * 1024
        ),
    )(cached_hidden, direction, expert_ids, gate_weights)
    gradient = lax.dot_general(
        adjoint.reshape(n_dp * rows, feat),
        rows_all.reshape(n_dp * rows, fw),
        (((0,), (0,)), ((), ())),
        preferred_element_type=jnp.float32,
    )
    return gradient.reshape(1, feat, fw)


def solution(mesh):
    return jax.shard_map(
        body,
        mesh=mesh,
        in_specs=(
            P(("dp", "expert"), None),
            P("expert", "dp", None),
            P(("dp", "expert"), None),
            P(("dp", "expert"), None),
        ),
        out_specs=P("expert", "dp", None),
        check_vma=False,
    )
```

```python
import functools
import math

import jax
import jax.numpy as jnp
from jax import lax
from jax.experimental import pallas as pl
from jax.experimental.pallas import tpu as pltpu
from jax.sharding import PartitionSpec as P

MESH = pl.DeviceIdType.MESH
CORES = 2
LANES = 128
CHUNKS = 2


def slot_positions(block_ids, experts):
    flat = block_ids.reshape(-1)
    onehot = (flat[:, None] == jnp.arange(experts, dtype=jnp.int32)[None, :]).astype(jnp.int32)
    before = jnp.cumsum(onehot, axis=0) - onehot
    return jnp.sum(before * onehot, axis=1).reshape(block_ids.shape)


def general_body(cached_hidden, direction, expert_ids, gate_weights):
    dp_count = lax.axis_size("dp")
    owner_count = lax.axis_size("expert")
    slot_rows = cached_hidden.shape[0]
    capacity = slot_rows // owner_count
    tok_count = expert_ids.shape[0]
    width = direction.shape[1] * dp_count
    local_dir = direction[0]
    rows_all = lax.all_gather(cached_hidden, "dp", axis=0, tiled=True)
    tangent = lax.dot_general(
        rows_all, local_dir, (((1,), (1,)), ((), ())), preferred_element_type=jnp.float32
    )
    tangent = tangent.astype(jnp.bfloat16).reshape(
        dp_count, owner_count, capacity, local_dir.shape[0]
    )
    returned = lax.all_to_all(
        lax.all_to_all(tangent, "dp", split_axis=0, concat_axis=3, tiled=True),
        "expert",
        split_axis=1,
        concat_axis=1,
        tiled=True,
    )
    flat_rows = returned.reshape(owner_count * capacity, width)
    treated = expert_ids < owner_count
    slot_pos = slot_positions(expert_ids, owner_count)
    target = expert_ids * capacity + slot_pos
    lookup = jnp.where(treated, target, 0).reshape(-1)
    dropped = jnp.where(treated, target, owner_count * capacity).reshape(-1)
    gates = jnp.where(treated, gate_weights, 0.0)
    picked = jnp.take(flat_rows, lookup, axis=0).reshape(tok_count, expert_ids.shape[1], width)
    scale_factor = 1.0 / math.sqrt(tok_count * dp_count * owner_count)
    combined = jnp.sum(gates[..., None] * picked.astype(jnp.float32), axis=1) * scale_factor
    outgoing = (gates[..., None] * combined[:, None, :]).astype(jnp.bfloat16)
    buffer = jnp.zeros((owner_count * capacity, width), jnp.bfloat16)
    buffer = buffer.at[dropped].set(outgoing.reshape(-1, width), mode="drop")
    buffer = buffer.reshape(1, owner_count, capacity, width)
    arrived = lax.all_to_all(buffer, "expert", split_axis=1, concat_axis=1, tiled=True)
    adjoint = lax.all_to_all(arrived, "dp", split_axis=3, concat_axis=0, tiled=True)
    adjoint_rows = adjoint.reshape(-1, adjoint.shape[3])
    gradient = lax.dot_general(
        adjoint_rows, rows_all, (((0,), (0,)), ((), ())), preferred_element_type=jnp.float32
    )
    return gradient.reshape(1, gradient.shape[0], gradient.shape[1])


def swap_blocks(x, cap):
    lane = lax.broadcasted_iota(jnp.int32, x.shape, 1)
    back = pltpu.roll(x, LANES - cap, 1)
    ahead = pltpu.roll(x, cap, 1)
    return jnp.where((lane // cap) % 2 == 0, back, ahead)


def pair_matrix(ids, gates, q, n_e, cap, scale):
    topk, toks = ids.shape
    slot = lax.broadcasted_iota(jnp.int32, (LANES, toks), 0)
    slot_e, slot_q, slot_c = slot // (n_e * cap), (slot // cap) % n_e, slot % cap
    named = jnp.zeros((LANES, toks), jnp.float32)
    gate = jnp.zeros((LANES, toks), jnp.float32)
    for k in range(topk):
        same = ids[k : k + 1, :] == slot_e
        named = named + jnp.where(same, 1.0, 0.0)
        gate = gate + jnp.where(same, gates[k : k + 1, :], 0.0)
    row = lax.broadcasted_iota(jnp.int32, (toks, toks), 0)
    col = lax.broadcasted_iota(jnp.int32, (toks, toks), 1)
    earlier = jnp.where(row < col, 1.0, 0.0).astype(jnp.bfloat16)
    position = jnp.dot(named.astype(jnp.bfloat16), earlier, preferred_element_type=jnp.float32)
    held = (position == slot_c.astype(jnp.float32)) & (slot_q == q)
    slots = jnp.where(held, gate, 0.0)
    high = slots.astype(jnp.bfloat16)
    low = (slots - high.astype(jnp.float32)).astype(jnp.bfloat16)
    nt = (((1,), (1,)), ((), ()))
    total = lax.dot_general(high, high, nt, preferred_element_type=jnp.float32)
    total += lax.dot_general(high, low, nt, preferred_element_type=jnp.float32)
    total += lax.dot_general(low, high, nt, preferred_element_type=jnp.float32)
    return total * scale


def kernel(
    n_dp, n_e, cap, scale,
    h_ref, dir_ref, ids_ref, gates_ref,
    adj_out, hall_out,
    adj, hall, dirv, idv, gatev, tang, pairs, wf, wall,
    loc_sem, out_sem, own_send, relay_send, hz_recv, hs_send, hs_recv,
    a_send, a_recv, w_send, w_recv, ws_send, ws_recv, t_send, t_recv,
):
    n_z = n_dp // CORES
    rows = n_e * cap
    feat = dirv.shape[0]
    part = rows // CHUNKS
    p = lax.axis_index("dp")
    e = lax.axis_index("expert")
    z, core = p // CORES, p % CORES
    sib = z * CORES + (1 - core)
    nt = (((1,), (1,)), ((), ()))

    load_dir = pltpu.make_async_copy(dir_ref.at[0], dirv, loc_sem.at[0])
    load_h = pltpu.make_async_copy(h_ref, hall.at[p], loc_sem.at[1])
    load_ids = pltpu.make_async_copy(ids_ref, idv, loc_sem.at[2])
    load_gates = pltpu.make_async_copy(gates_ref, gatev, loc_sem.at[3])
    load_ids.start()
    load_gates.start()
    load_h.start()
    load_dir.start()

    def z_peer(d):
        return lax.rem(z + d, n_z)

    def e_peer(d):
        return lax.rem(e + d, n_e)

    barrier = pltpu.get_barrier_semaphore()
    for d in range(1, n_z):
        pl.semaphore_signal(barrier, inc=1, device_id=(z_peer(d) * CORES + core, e), device_id_type=MESH)
    for d in range(1, n_e):
        pl.semaphore_signal(barrier, inc=1, device_id=(p, e_peer(d)), device_id_type=MESH)
    pl.semaphore_signal(barrier, inc=1, device_id=(sib, e), device_id_type=MESH)
    mine = pl.ds(pl.multiple_of(e * rows, rows), rows)
    tang[:, mine, feat // LANES * LANES :] = jnp.zeros(
        (n_dp, rows, tang.shape[2] - feat // LANES * LANES), jnp.bfloat16
    )
    pl.semaphore_wait(barrier, n_z + n_e - 1)

    def remote(src, dst, send, recv, dev):
        return pltpu.make_async_remote_copy(
            src_ref=src, dst_ref=dst, send_sem=send, recv_sem=recv, device_id=dev, device_id_type=MESH
        )

    def own_copy(side, c):
        to = z + 1 if side == 0 else z - 1
        return remote(
            h_ref.at[pl.ds(c * part, part)], hall.at[p, pl.ds(c * part, part)],
            own_send.at[side, c], hz_recv.at[z, c], (to * CORES + core, e),
        )

    def on_side(side, fn):
        pl.when(z + 1 < n_z if side == 0 else z > 0)(fn)

    for c in range(CHUNKS):
        for side in range(2):
            on_side(side, lambda side=side, c=c: own_copy(side, c).start())

    def sibling_copy(zs, src):
        row = zs * CORES + core
        return remote(src, hall.at[row], hs_send.at[zs], hs_recv.at[zs], (sib, e))

    sibling_copy(z, h_ref).start()

    load_ids.wait()
    load_gates.wait()
    pairs[...] = pair_matrix(idv[...], gatev[...], e, n_e, cap, scale)

    def slot_rows(owner, source):
        return pl.ds(pl.multiple_of(owner * rows + source * cap, cap), cap)

    def pair_copy(d):
        to = e_peer(d)
        return remote(
            pairs.at[slot_rows(to, e)], wf.at[pl.ds(pl.multiple_of(e * cap, cap), cap)],
            a_send.at[d], a_recv.at[e], (p, to),
        )

    for d in range(1, n_e):
        pair_copy(d).start()
    wf[pl.ds(pl.multiple_of(e * cap, cap), cap), :] = pairs[slot_rows(e, e), :]

    def tangent_copy(zs, d):
        ref = tang.at[pl.ds(zs * CORES, CORES), mine]
        return remote(ref, ref, t_send.at[zs, d], t_recv.at[zs, e], (p, e_peer(d)))

    def rows_out(zs):
        two = pl.ds(zs * CORES, CORES)
        return pltpu.make_async_copy(hall.at[two], hall_out.at[two], out_sem.at[0, zs])

    def tangents(zs):
        rows_out(zs).start()
        block = hall[pl.ds(zs * CORES, CORES)].reshape(CORES * rows, hall.shape[2])
        out = lax.dot_general(block, dirv[...], nt, preferred_element_type=jnp.float32)
        tang[pl.ds(zs * CORES, CORES), mine, :feat] = out.astype(jnp.bfloat16).reshape(CORES, rows, feat)
        for d in range(1, n_e):
            tangent_copy(zs, d).start()

    load_dir.wait()
    load_h.wait()
    sibling_copy(z, h_ref).wait_recv()
    tangents(z)

    def weight_copy(d):
        return remote(wall.at[p], wall.at[p], w_send.at[d], w_recv.at[z], (z_peer(d) * CORES + core, e))

    def weight_sibling(zs):
        ref = wall.at[zs * CORES + core]
        return remote(ref, ref, ws_send.at[zs], ws_recv.at[zs], (sib, e))

    def share_weights():
        for d in range(1, n_e):
            src = e_peer(d)
            remote(
                pairs.at[slot_rows(e, src)], wf.at[pl.ds(pl.multiple_of(src * cap, cap), cap)],
                a_send.at[d], a_recv.at[src], (p, src),
            ).wait_recv()
        weights = wf[...]
        high = weights.astype(jnp.bfloat16).astype(jnp.float32)
        wall[p] = (high + swap_blocks(weights - high, cap)).astype(jnp.bfloat16)
        for d in range(1, n_z):
            weight_copy(d).start()
        weight_sibling(z).start()

    def forward_weights(zs):
        ref = wall.at[zs * CORES + core]
        remote(ref, ref, w_send.at[1], w_recv.at[zs], (sib, e)).wait_recv()
        weight_sibling(zs).start()

    near = jnp.minimum(z, n_z - 1 - z)

    def source(j):
        if j == 0:
            return z
        s = (j + 1) // 2
        close = z - s if j % 2 else z + s
        far = jnp.where(2 * z < n_z - 1, j, n_z - 1 - j)
        return jnp.where(j <= 2 * near, close, far)

    def relay_copy(zs, c):
        to = jnp.where(zs < z, z + 1, z - 1)
        ref = hall.at[zs * CORES + core, pl.ds(c * part, part)]
        return remote(ref, ref, relay_send.at[zs, c], hz_recv.at[zs, c], (to * CORES + core, e))

    def relays(zs, fn):
        to = jnp.where(zs < z, z + 1, z - 1)
        pl.when((to >= 0) & (to < n_z))(fn)

    lane = lax.broadcasted_iota(jnp.int32, (rows, LANES), 1)
    row = lax.broadcasted_iota(jnp.int32, (rows, LANES), 0)
    direct = (lane // cap) % n_e == row // cap

    def adjoint_out(zs):
        two = pl.ds(zs * CORES, CORES)
        return pltpu.make_async_copy(adj.at[two], adj_out.at[two], out_sem.at[1, zs])

    def finish(zs):
        weight_sibling(zs).wait_recv()
        for d in range(1, n_e):
            src = e_peer(d)
            ref = tang.at[pl.ds(zs * CORES, CORES), pl.ds(pl.multiple_of(src * rows, rows), rows)]
            remote(ref, ref, t_send.at[zs, d], t_recv.at[zs, src], (p, src)).wait_recv()
        for k in range(CORES):
            packed = wall[zs * CORES + k].astype(jnp.float32)
            high = jnp.where(direct, packed, 0.0)
            low = swap_blocks(packed - high, cap)
            both = jnp.concatenate([high, low], axis=0).astype(jnp.bfloat16)
            out = jnp.dot(both, tang[zs * CORES + k], preferred_element_type=jnp.float32)
            out = (out[:rows] + out[rows:]).astype(jnp.bfloat16)
            adj[zs * CORES + k] = out[:, :feat]
        adjoint_out(zs).start()

    for j in range(1, n_z):
        zs = source(j)
        for c in range(CHUNKS):
            relay_copy(zs, c).wait_recv()
            relays(zs, lambda zs=zs, c=c: relay_copy(zs, c).start())
        sibling_copy(zs, hall.at[zs * CORES + core]).start()
        if j == 1:
            share_weights()
        sibling_copy(zs, hall.at[zs * CORES + core]).wait_recv()
        tangents(zs)
        if j >= 2:
            forward_weights(source(j - 1))
            finish(source(j - 2))
    forward_weights(source(n_z - 1))
    finish(source(n_z - 2))
    finish(source(n_z - 1))

    for c in range(CHUNKS):
        for side in range(2):
            on_side(side, lambda side=side, c=c: own_copy(side, c).wait_send())
    for d in range(1, n_e):
        pair_copy(d).wait_send()
    for d in range(1, n_z):
        weight_copy(d).wait_send()
    for j in range(n_z):
        zs = source(j)
        adjoint_out(zs).wait()
        rows_out(zs).wait()
        sibling_copy(zs, hall.at[zs * CORES + core]).wait_send()
        weight_sibling(zs).wait_send()
        for d in range(1, n_e):
            tangent_copy(zs, d).wait_send()
        if j:
            for c in range(CHUNKS):
                relays(zs, lambda zs=zs, c=c: relay_copy(zs, c).wait_send())


def body(cached_hidden, direction, expert_ids, gate_weights):
    n_dp, n_e = lax.axis_size("dp"), lax.axis_size("expert")
    rows, fw = cached_hidden.shape
    cap = rows // n_e
    feat = direction.shape[1]
    if n_e * rows != LANES or cap % 8 or rows % (16 * CHUNKS) or n_dp % CORES or n_dp < 2 * CORES:
        return general_body(cached_hidden, direction, expert_ids, gate_weights)
    n_z = n_dp // CORES
    wide = -(-feat // LANES) * LANES
    scale = 1.0 / math.sqrt(expert_ids.shape[0] * n_dp * n_e)
    hbm = pl.BlockSpec(memory_space=pltpu.HBM)
    dma = pltpu.SemaphoreType.DMA
    adjoint, rows_all = pl.pallas_call(
        functools.partial(kernel, n_dp, n_e, cap, scale),
        out_shape=(
            jax.ShapeDtypeStruct((n_dp, rows, feat), jnp.bfloat16),
            jax.ShapeDtypeStruct((n_dp, rows, fw), jnp.bfloat16),
        ),
        in_specs=[hbm] * 4,
        out_specs=(hbm, hbm),
        scratch_shapes=[
            pltpu.VMEM((n_dp, rows, feat), jnp.bfloat16),
            pltpu.VMEM((n_dp, rows, fw), jnp.bfloat16),
            pltpu.VMEM((feat, fw), jnp.bfloat16),
            pltpu.VMEM(expert_ids.shape[::-1], jnp.int32),
            pltpu.VMEM(gate_weights.shape[::-1], jnp.float32),
            pltpu.VMEM((n_dp, n_e * rows, wide), jnp.bfloat16),
            pltpu.VMEM((LANES, LANES), jnp.float32),
            pltpu.VMEM((rows, LANES), jnp.float32),
            pltpu.VMEM((n_dp, rows, LANES), jnp.bfloat16),
            dma((4,)),
            dma((2, n_z)),
            dma((2, CHUNKS)),
            dma((n_z, CHUNKS)),
            dma((n_z, CHUNKS)),
            dma((n_z,)),
            dma((n_z,)),
            dma((n_e,)),
            dma((n_e,)),
            dma((n_z,)),
            dma((n_z,)),
            dma((n_z,)),
            dma((n_z,)),
            dma((n_z, n_e)),
            dma((n_z, n_e)),
        ],
        compiler_params=pltpu.CompilerParams(
            collective_id=0, has_side_effects=True, vmem_limit_bytes=56 * 1024 * 1024
        ),
    )(cached_hidden, direction, expert_ids.T, gate_weights.T)
    gradient = lax.dot_general(
        adjoint.reshape(n_dp * rows, feat),
        rows_all.reshape(n_dp * rows, fw),
        (((0,), (0,)), ((), ())),
        preferred_element_type=jnp.float32,
    )
    return gradient.reshape(1, feat, fw)


def solution(mesh):
    return jax.shard_map(
        body,
        mesh=mesh,
        in_specs=(
            P(("dp", "expert"), None),
            P("expert", "dp", None),
            P(("dp", "expert"), None),
            P(("dp", "expert"), None),
        ),
        out_specs=P("expert", "dp", None),
        check_vma=False,
    )
```

```python
import functools
import math

import jax
import jax.numpy as jnp
from jax import lax
from jax.experimental import pallas as pl
from jax.experimental.pallas import tpu as pltpu
from jax.sharding import PartitionSpec as P

MESH = pl.DeviceIdType.MESH
CORES = 2
LANES = 128
CHUNKS = 2


def slot_positions(block_ids, experts):
    flat = block_ids.reshape(-1)
    onehot = (flat[:, None] == jnp.arange(experts, dtype=jnp.int32)[None, :]).astype(jnp.int32)
    before = jnp.cumsum(onehot, axis=0) - onehot
    return jnp.sum(before * onehot, axis=1).reshape(block_ids.shape)


def general_body(cached_hidden, direction, expert_ids, gate_weights):
    dp_count = lax.axis_size("dp")
    owner_count = lax.axis_size("expert")
    slot_rows = cached_hidden.shape[0]
    capacity = slot_rows // owner_count
    tok_count = expert_ids.shape[0]
    width = direction.shape[1] * dp_count
    local_dir = direction[0]
    rows_all = lax.all_gather(cached_hidden, "dp", axis=0, tiled=True)
    tangent = lax.dot_general(
        rows_all, local_dir, (((1,), (1,)), ((), ())), preferred_element_type=jnp.float32
    )
    tangent = tangent.astype(jnp.bfloat16).reshape(
        dp_count, owner_count, capacity, local_dir.shape[0]
    )
    returned = lax.all_to_all(
        lax.all_to_all(tangent, "dp", split_axis=0, concat_axis=3, tiled=True),
        "expert",
        split_axis=1,
        concat_axis=1,
        tiled=True,
    )
    flat_rows = returned.reshape(owner_count * capacity, width)
    treated = expert_ids < owner_count
    slot_pos = slot_positions(expert_ids, owner_count)
    target = expert_ids * capacity + slot_pos
    lookup = jnp.where(treated, target, 0).reshape(-1)
    dropped = jnp.where(treated, target, owner_count * capacity).reshape(-1)
    gates = jnp.where(treated, gate_weights, 0.0)
    picked = jnp.take(flat_rows, lookup, axis=0).reshape(tok_count, expert_ids.shape[1], width)
    scale_factor = 1.0 / math.sqrt(tok_count * dp_count * owner_count)
    combined = jnp.sum(gates[..., None] * picked.astype(jnp.float32), axis=1) * scale_factor
    outgoing = (gates[..., None] * combined[:, None, :]).astype(jnp.bfloat16)
    buffer = jnp.zeros((owner_count * capacity, width), jnp.bfloat16)
    buffer = buffer.at[dropped].set(outgoing.reshape(-1, width), mode="drop")
    buffer = buffer.reshape(1, owner_count, capacity, width)
    arrived = lax.all_to_all(buffer, "expert", split_axis=1, concat_axis=1, tiled=True)
    adjoint = lax.all_to_all(arrived, "dp", split_axis=3, concat_axis=0, tiled=True)
    adjoint_rows = adjoint.reshape(-1, adjoint.shape[3])
    gradient = lax.dot_general(
        adjoint_rows, rows_all, (((0,), (0,)), ((), ())), preferred_element_type=jnp.float32
    )
    return gradient.reshape(1, gradient.shape[0], gradient.shape[1])


def swap_blocks(x, cap):
    lane = lax.broadcasted_iota(jnp.int32, x.shape, 1)
    back = pltpu.roll(x, LANES - cap, 1)
    ahead = pltpu.roll(x, cap, 1)
    return jnp.where((lane // cap) % 2 == 0, back, ahead)


def pair_matrix(ids, gates, q, n_e, cap, scale):
    topk, toks = ids.shape
    slot = lax.broadcasted_iota(jnp.int32, (LANES, toks), 0)
    slot_e, slot_q, slot_c = slot // (n_e * cap), (slot // cap) % n_e, slot % cap
    named = jnp.zeros((LANES, toks), jnp.float32)
    gate = jnp.zeros((LANES, toks), jnp.float32)
    for k in range(topk):
        same = ids[k : k + 1, :] == slot_e
        named = named + jnp.where(same, 1.0, 0.0)
        gate = gate + jnp.where(same, gates[k : k + 1, :], 0.0)
    row = lax.broadcasted_iota(jnp.int32, (toks, toks), 0)
    col = lax.broadcasted_iota(jnp.int32, (toks, toks), 1)
    earlier = jnp.where(row < col, 1.0, 0.0).astype(jnp.bfloat16)
    position = jnp.dot(named.astype(jnp.bfloat16), earlier, preferred_element_type=jnp.float32)
    held = (position == slot_c.astype(jnp.float32)) & (slot_q == q)
    slots = jnp.where(held, gate, 0.0)
    high = slots.astype(jnp.bfloat16)
    low = (slots - high.astype(jnp.float32)).astype(jnp.bfloat16)
    nt = (((1,), (1,)), ((), ()))
    total = lax.dot_general(high, high, nt, preferred_element_type=jnp.float32)
    total += lax.dot_general(high, low, nt, preferred_element_type=jnp.float32)
    total += lax.dot_general(low, high, nt, preferred_element_type=jnp.float32)
    return total * scale


def kernel(
    n_dp, n_e, cap, scale,
    h_ref, dir_ref, ids_ref, gates_ref,
    adj_out, hall_out,
    adj, hall, dirv, idv, gatev, tang, pairs, wf, wall,
    loc_sem, out_sem, own_send, far_send, relay_send, hz_recv, hs_send, hs_recv,
    a_send, a_recv, w_send, w_recv, ws_send, ws_recv, t_send, t_recv,
):
    n_z = n_dp // CORES
    rows = n_e * cap
    feat = dirv.shape[0]
    part = rows // CHUNKS
    p = lax.axis_index("dp")
    e = lax.axis_index("expert")
    z, core = p // CORES, p % CORES
    sib = z * CORES + (1 - core)
    nt = (((1,), (1,)), ((), ()))

    load_dir = pltpu.make_async_copy(dir_ref.at[0], dirv, loc_sem.at[0])
    load_h = pltpu.make_async_copy(h_ref, hall.at[p], loc_sem.at[1])
    load_ids = pltpu.make_async_copy(ids_ref, idv, loc_sem.at[2])
    load_gates = pltpu.make_async_copy(gates_ref, gatev, loc_sem.at[3])
    load_ids.start()
    load_gates.start()
    load_h.start()
    load_dir.start()

    def z_peer(d):
        return lax.rem(z + d, n_z)

    def e_peer(d):
        return lax.rem(e + d, n_e)

    barrier = pltpu.get_barrier_semaphore()
    for d in range(1, n_z):
        pl.semaphore_signal(barrier, inc=1, device_id=(z_peer(d) * CORES + core, e), device_id_type=MESH)
    for d in range(1, n_e):
        pl.semaphore_signal(barrier, inc=1, device_id=(p, e_peer(d)), device_id_type=MESH)
    pl.semaphore_signal(barrier, inc=1, device_id=(sib, e), device_id_type=MESH)
    mine = pl.ds(pl.multiple_of(e * rows, rows), rows)
    tang[:, mine, feat // LANES * LANES :] = jnp.zeros(
        (n_dp, rows, tang.shape[2] - feat // LANES * LANES), jnp.bfloat16
    )
    pl.semaphore_wait(barrier, n_z + n_e - 1)

    def remote(src, dst, send, recv, dev):
        return pltpu.make_async_remote_copy(
            src_ref=src, dst_ref=dst, send_sem=send, recv_sem=recv, device_id=dev, device_id_type=MESH
        )

    def own_copy(side, c):
        to = z + 1 if side == 0 else z - 1
        return remote(
            h_ref.at[pl.ds(c * part, part)], hall.at[p, pl.ds(c * part, part)],
            own_send.at[side, c], hz_recv.at[z, c], (to * CORES + core, e),
        )

    def on_side(side, fn):
        pl.when(z + 1 < n_z if side == 0 else z > 0)(fn)

    for c in range(CHUNKS):
        for side in range(2):
            on_side(side, lambda side=side, c=c: own_copy(side, c).start())

    at_end = (z == 0) | (z == n_z - 1)

    def far_copy(d, c):
        to = jnp.where(z == 0, d, n_z - 1 - d)
        return remote(
            h_ref.at[pl.ds(c * part, part)], hall.at[p, pl.ds(c * part, part)],
            far_send.at[d, c], hz_recv.at[z, c], (to * CORES + core, e),
        )

    def far(d, act):
        def both():
            for c in range(CHUNKS):
                act(far_copy(d, c))

        pl.when(at_end)(both)

    def sibling_copy(zs, src):
        row = zs * CORES + core
        return remote(src, hall.at[row], hs_send.at[zs], hs_recv.at[zs], (sib, e))

    sibling_copy(z, h_ref).start()

    load_ids.wait()
    load_gates.wait()
    pairs[...] = pair_matrix(idv[...], gatev[...], e, n_e, cap, scale)

    def slot_rows(owner, source):
        return pl.ds(pl.multiple_of(owner * rows + source * cap, cap), cap)

    def pair_copy(d):
        to = e_peer(d)
        return remote(
            pairs.at[slot_rows(to, e)], wf.at[pl.ds(pl.multiple_of(e * cap, cap), cap)],
            a_send.at[d], a_recv.at[e], (p, to),
        )

    for d in range(1, n_e):
        pair_copy(d).start()
    far(2, lambda copy: copy.start())
    wf[pl.ds(pl.multiple_of(e * cap, cap), cap), :] = pairs[slot_rows(e, e), :]

    def tangent_copy(zs, d):
        ref = tang.at[pl.ds(zs * CORES, CORES), mine]
        return remote(ref, ref, t_send.at[zs, d], t_recv.at[zs, e], (p, e_peer(d)))

    def rows_out(zs):
        two = pl.ds(zs * CORES, CORES)
        return pltpu.make_async_copy(hall.at[two], hall_out.at[two], out_sem.at[0, zs])

    def tangents(zs):
        rows_out(zs).start()
        block = hall[pl.ds(zs * CORES, CORES)].reshape(CORES * rows, hall.shape[2])
        out = lax.dot_general(block, dirv[...], nt, preferred_element_type=jnp.float32)
        tang[pl.ds(zs * CORES, CORES), mine, :feat] = out.astype(jnp.bfloat16).reshape(CORES, rows, feat)
        for d in range(1, n_e):
            tangent_copy(zs, d).start()

    load_dir.wait()
    load_h.wait()
    sibling_copy(z, h_ref).wait_recv()
    tangents(z)

    def weight_copy(d):
        return remote(wall.at[p], wall.at[p], w_send.at[d], w_recv.at[z], (z_peer(d) * CORES + core, e))

    def weight_sibling(zs):
        ref = wall.at[zs * CORES + core]
        return remote(ref, ref, ws_send.at[zs], ws_recv.at[zs], (sib, e))

    def share_weights():
        for d in range(1, n_e):
            src = e_peer(d)
            remote(
                pairs.at[slot_rows(e, src)], wf.at[pl.ds(pl.multiple_of(src * cap, cap), cap)],
                a_send.at[d], a_recv.at[src], (p, src),
            ).wait_recv()
        weights = wf[...]
        high = weights.astype(jnp.bfloat16).astype(jnp.float32)
        wall[p] = (high + swap_blocks(weights - high, cap)).astype(jnp.bfloat16)
        for d in range(1, n_z):
            weight_copy(d).start()
        weight_sibling(z).start()

    def forward_weights(zs):
        ref = wall.at[zs * CORES + core]
        remote(ref, ref, w_send.at[1], w_recv.at[zs], (sib, e)).wait_recv()
        weight_sibling(zs).start()

    near = jnp.minimum(z, n_z - 1 - z)

    def source(j):
        if j == 0:
            return z
        s = (j + 1) // 2
        close = z - s if j % 2 else z + s
        far = jnp.where(2 * z < n_z - 1, j, n_z - 1 - j)
        return jnp.where(j <= 2 * near, close, far)

    def relay_copy(zs, c):
        to = jnp.where(zs < z, z + 1, z - 1)
        ref = hall.at[zs * CORES + core, pl.ds(c * part, part)]
        return remote(ref, ref, relay_send.at[zs, c], hz_recv.at[zs, c], (to * CORES + core, e))

    def relays(zs, fn):
        to = jnp.where(zs < z, z + 1, z - 1)
        pl.when((to >= 0) & (to < n_z) & (zs > 0) & (zs < n_z - 1))(fn)

    lane = lax.broadcasted_iota(jnp.int32, (rows, LANES), 1)
    row = lax.broadcasted_iota(jnp.int32, (rows, LANES), 0)
    direct = (lane // cap) % n_e == row // cap

    def adjoint_out(zs):
        two = pl.ds(zs * CORES, CORES)
        return pltpu.make_async_copy(adj.at[two], adj_out.at[two], out_sem.at[1, zs])

    def finish(zs):
        weight_sibling(zs).wait_recv()
        for d in range(1, n_e):
            src = e_peer(d)
            ref = tang.at[pl.ds(zs * CORES, CORES), pl.ds(pl.multiple_of(src * rows, rows), rows)]
            remote(ref, ref, t_send.at[zs, d], t_recv.at[zs, src], (p, src)).wait_recv()
        for k in range(CORES):
            packed = wall[zs * CORES + k].astype(jnp.float32)
            high = jnp.where(direct, packed, 0.0)
            low = swap_blocks(packed - high, cap)
            both = jnp.concatenate([high, low], axis=0).astype(jnp.bfloat16)
            out = jnp.dot(both, tang[zs * CORES + k], preferred_element_type=jnp.float32)
            out = (out[:rows] + out[rows:]).astype(jnp.bfloat16)
            adj[zs * CORES + k] = out[:, :feat]
        adjoint_out(zs).start()

    for j in range(1, n_z):
        zs = source(j)
        for c in range(CHUNKS):
            relay_copy(zs, c).wait_recv()
            relays(zs, lambda zs=zs, c=c: relay_copy(zs, c).start())
        sibling_copy(zs, hall.at[zs * CORES + core]).start()
        if j + 2 < n_z:
            far(j + 2, lambda copy: copy.start())
        if j == 1:
            share_weights()
        sibling_copy(zs, hall.at[zs * CORES + core]).wait_recv()
        tangents(zs)
        if j >= 2:
            forward_weights(source(j - 1))
            finish(source(j - 2))
    forward_weights(source(n_z - 1))
    finish(source(n_z - 2))
    finish(source(n_z - 1))

    for c in range(CHUNKS):
        for side in range(2):
            on_side(side, lambda side=side, c=c: own_copy(side, c).wait_send())
    for d in range(2, n_z):
        far(d, lambda copy: copy.wait_send())
    for d in range(1, n_e):
        pair_copy(d).wait_send()
    for d in range(1, n_z):
        weight_copy(d).wait_send()
    for j in range(n_z):
        zs = source(j)
        adjoint_out(zs).wait()
        rows_out(zs).wait()
        sibling_copy(zs, hall.at[zs * CORES + core]).wait_send()
        weight_sibling(zs).wait_send()
        for d in range(1, n_e):
            tangent_copy(zs, d).wait_send()
        if j:
            for c in range(CHUNKS):
                relays(zs, lambda zs=zs, c=c: relay_copy(zs, c).wait_send())


def body(cached_hidden, direction, expert_ids, gate_weights):
    n_dp, n_e = lax.axis_size("dp"), lax.axis_size("expert")
    rows, fw = cached_hidden.shape
    cap = rows // n_e
    feat = direction.shape[1]
    if n_e * rows != LANES or cap % 8 or rows % (16 * CHUNKS) or n_dp % CORES or n_dp < 3 * CORES:
        return general_body(cached_hidden, direction, expert_ids, gate_weights)
    n_z = n_dp // CORES
    wide = -(-feat // LANES) * LANES
    scale = 1.0 / math.sqrt(expert_ids.shape[0] * n_dp * n_e)
    hbm = pl.BlockSpec(memory_space=pltpu.HBM)
    dma = pltpu.SemaphoreType.DMA
    adjoint, rows_all = pl.pallas_call(
        functools.partial(kernel, n_dp, n_e, cap, scale),
        out_shape=(
            jax.ShapeDtypeStruct((n_dp, rows, feat), jnp.bfloat16),
            jax.ShapeDtypeStruct((n_dp, rows, fw), jnp.bfloat16),
        ),
        in_specs=[hbm] * 4,
        out_specs=(hbm, hbm),
        scratch_shapes=[
            pltpu.VMEM((n_dp, rows, feat), jnp.bfloat16),
            pltpu.VMEM((n_dp, rows, fw), jnp.bfloat16),
            pltpu.VMEM((feat, fw), jnp.bfloat16),
            pltpu.VMEM(expert_ids.shape[::-1], jnp.int32),
            pltpu.VMEM(gate_weights.shape[::-1], jnp.float32),
            pltpu.VMEM((n_dp, n_e * rows, wide), jnp.bfloat16),
            pltpu.VMEM((LANES, LANES), jnp.float32),
            pltpu.VMEM((rows, LANES), jnp.float32),
            pltpu.VMEM((n_dp, rows, LANES), jnp.bfloat16),
            dma((4,)),
            dma((2, n_z)),
            dma((2, CHUNKS)),
            dma((n_z, CHUNKS)),
            dma((n_z, CHUNKS)),
            dma((n_z, CHUNKS)),
            dma((n_z,)),
            dma((n_z,)),
            dma((n_e,)),
            dma((n_e,)),
            dma((n_z,)),
            dma((n_z,)),
            dma((n_z,)),
            dma((n_z,)),
            dma((n_z, n_e)),
            dma((n_z, n_e)),
        ],
        compiler_params=pltpu.CompilerParams(
            collective_id=0, has_side_effects=True, vmem_limit_bytes=56 * 1024 * 1024
        ),
    )(cached_hidden, direction, expert_ids.T, gate_weights.T)
    gradient = lax.dot_general(
        adjoint.reshape(n_dp * rows, feat),
        rows_all.reshape(n_dp * rows, fw),
        (((0,), (0,)), ((), ())),
        preferred_element_type=jnp.float32,
    )
    return gradient.reshape(1, feat, fw)


def solution(mesh):
    return jax.shard_map(
        body,
        mesh=mesh,
        in_specs=(
            P(("dp", "expert"), None),
            P("expert", "dp", None),
            P(("dp", "expert"), None),
            P(("dp", "expert"), None),
        ),
        out_specs=P("expert", "dp", None),
        check_vma=False,
    )
```

```python
import functools
import math

import jax
import jax.numpy as jnp
from jax import lax
from jax.experimental import pallas as pl
from jax.experimental.pallas import tpu as pltpu
from jax.sharding import PartitionSpec as P

MESH = pl.DeviceIdType.MESH
CORES = 2
LANES = 128
CHUNKS = 2


def slot_positions(block_ids, experts):
    flat = block_ids.reshape(-1)
    onehot = (flat[:, None] == jnp.arange(experts, dtype=jnp.int32)[None, :]).astype(jnp.int32)
    before = jnp.cumsum(onehot, axis=0) - onehot
    return jnp.sum(before * onehot, axis=1).reshape(block_ids.shape)


def general_body(cached_hidden, direction, expert_ids, gate_weights):
    dp_count = lax.axis_size("dp")
    owner_count = lax.axis_size("expert")
    slot_rows = cached_hidden.shape[0]
    capacity = slot_rows // owner_count
    tok_count = expert_ids.shape[0]
    width = direction.shape[1] * dp_count
    local_dir = direction[0]
    rows_all = lax.all_gather(cached_hidden, "dp", axis=0, tiled=True)
    tangent = lax.dot_general(
        rows_all, local_dir, (((1,), (1,)), ((), ())), preferred_element_type=jnp.float32
    )
    tangent = tangent.astype(jnp.bfloat16).reshape(
        dp_count, owner_count, capacity, local_dir.shape[0]
    )
    returned = lax.all_to_all(
        lax.all_to_all(tangent, "dp", split_axis=0, concat_axis=3, tiled=True),
        "expert",
        split_axis=1,
        concat_axis=1,
        tiled=True,
    )
    flat_rows = returned.reshape(owner_count * capacity, width)
    treated = expert_ids < owner_count
    slot_pos = slot_positions(expert_ids, owner_count)
    target = expert_ids * capacity + slot_pos
    lookup = jnp.where(treated, target, 0).reshape(-1)
    dropped = jnp.where(treated, target, owner_count * capacity).reshape(-1)
    gates = jnp.where(treated, gate_weights, 0.0)
    picked = jnp.take(flat_rows, lookup, axis=0).reshape(tok_count, expert_ids.shape[1], width)
    scale_factor = 1.0 / math.sqrt(tok_count * dp_count * owner_count)
    combined = jnp.sum(gates[..., None] * picked.astype(jnp.float32), axis=1) * scale_factor
    outgoing = (gates[..., None] * combined[:, None, :]).astype(jnp.bfloat16)
    buffer = jnp.zeros((owner_count * capacity, width), jnp.bfloat16)
    buffer = buffer.at[dropped].set(outgoing.reshape(-1, width), mode="drop")
    buffer = buffer.reshape(1, owner_count, capacity, width)
    arrived = lax.all_to_all(buffer, "expert", split_axis=1, concat_axis=1, tiled=True)
    adjoint = lax.all_to_all(arrived, "dp", split_axis=3, concat_axis=0, tiled=True)
    adjoint_rows = adjoint.reshape(-1, adjoint.shape[3])
    gradient = lax.dot_general(
        adjoint_rows, rows_all, (((0,), (0,)), ((), ())), preferred_element_type=jnp.float32
    )
    return gradient.reshape(1, gradient.shape[0], gradient.shape[1])


def swap_blocks(x, cap):
    lane = lax.broadcasted_iota(jnp.int32, x.shape, 1)
    back = pltpu.roll(x, LANES - cap, 1)
    ahead = pltpu.roll(x, cap, 1)
    return jnp.where((lane // cap) % 2 == 0, back, ahead)


def pair_matrix(ids, gates, q, n_e, cap, scale):
    topk, toks = ids.shape
    slot = lax.broadcasted_iota(jnp.int32, (LANES, toks), 0)
    slot_e, slot_q, slot_c = slot // (n_e * cap), (slot // cap) % n_e, slot % cap
    named = jnp.zeros((LANES, toks), jnp.float32)
    gate = jnp.zeros((LANES, toks), jnp.float32)
    for k in range(topk):
        same = ids[k : k + 1, :] == slot_e
        named = named + jnp.where(same, 1.0, 0.0)
        gate = gate + jnp.where(same, gates[k : k + 1, :], 0.0)
    row = lax.broadcasted_iota(jnp.int32, (toks, toks), 0)
    col = lax.broadcasted_iota(jnp.int32, (toks, toks), 1)
    earlier = jnp.where(row < col, 1.0, 0.0).astype(jnp.bfloat16)
    position = jnp.dot(named.astype(jnp.bfloat16), earlier, preferred_element_type=jnp.float32)
    held = (position == slot_c.astype(jnp.float32)) & (slot_q == q)
    slots = jnp.where(held, gate, 0.0)
    high = slots.astype(jnp.bfloat16)
    low = (slots - high.astype(jnp.float32)).astype(jnp.bfloat16)
    nt = (((1,), (1,)), ((), ()))
    total = lax.dot_general(high, high, nt, preferred_element_type=jnp.float32)
    total += lax.dot_general(high, low, nt, preferred_element_type=jnp.float32)
    total += lax.dot_general(low, high, nt, preferred_element_type=jnp.float32)
    return total * scale


def kernel(
    n_dp, n_e, cap, scale,
    h_ref, dir_ref, ids_ref, gates_ref,
    adj_out, hall_out,
    adj, hall, dirv, idv, gatev, tang, pairs, wf, wall,
    loc_sem, out_sem, own_send, relay_send, hz_recv, hs_send, hs_recv,
    a_send, a_recv, w_send, w_recv, ws_send, ws_recv, t_send, t_recv, o_send, o_recv,
):
    n_z = n_dp // CORES
    rows = n_e * cap
    feat = dirv.shape[0]
    part = rows // CHUNKS
    p = lax.axis_index("dp")
    e = lax.axis_index("expert")
    z, core = p // CORES, p % CORES
    sib = z * CORES + (1 - core)
    nt = (((1,), (1,)), ((), ()))

    load_dir = pltpu.make_async_copy(dir_ref.at[0], dirv, loc_sem.at[0])
    load_h = pltpu.make_async_copy(h_ref, hall.at[p], loc_sem.at[1])
    load_ids = pltpu.make_async_copy(ids_ref, idv, loc_sem.at[2])
    load_gates = pltpu.make_async_copy(gates_ref, gatev, loc_sem.at[3])
    load_ids.start()
    load_gates.start()
    load_h.start()
    load_dir.start()

    def z_peer(d):
        return lax.rem(z + d, n_z)

    def e_peer(d):
        return lax.rem(e + d, n_e)

    barrier = pltpu.get_barrier_semaphore()
    for d in range(1, n_z):
        pl.semaphore_signal(barrier, inc=1, device_id=(z_peer(d) * CORES + core, e), device_id_type=MESH)
    for d in range(1, n_e):
        pl.semaphore_signal(barrier, inc=1, device_id=(p, e_peer(d)), device_id_type=MESH)
    pl.semaphore_signal(barrier, inc=1, device_id=(sib, e), device_id_type=MESH)
    mine = pl.ds(pl.multiple_of(e * rows, rows), rows)
    tang[:, mine, feat // LANES * LANES :] = jnp.zeros(
        (n_dp, rows, tang.shape[2] - feat // LANES * LANES), jnp.bfloat16
    )
    pl.semaphore_wait(barrier, n_z + n_e - 1)

    def remote(src, dst, send, recv, dev):
        return pltpu.make_async_remote_copy(
            src_ref=src, dst_ref=dst, send_sem=send, recv_sem=recv, device_id=dev, device_id_type=MESH
        )

    def own_copy(side, c):
        to = z + 1 if side == 0 else z - 1
        return remote(
            h_ref.at[pl.ds(c * part, part)], hall.at[p, pl.ds(c * part, part)],
            own_send.at[side, c], hz_recv.at[z, c], (to * CORES + core, e),
        )

    def on_side(side, fn):
        pl.when(z + 1 < n_z if side == 0 else z > 0)(fn)

    for c in range(CHUNKS):
        for side in range(2):
            on_side(side, lambda side=side, c=c: own_copy(side, c).start())

    def sibling_copy(zs, src):
        row = zs * CORES + core
        return remote(src, hall.at[row], hs_send.at[zs], hs_recv.at[zs], (sib, e))

    sibling_copy(z, h_ref).start()

    load_ids.wait()
    load_gates.wait()
    pairs[...] = pair_matrix(idv[...], gatev[...], e, n_e, cap, scale)

    def slot_rows(owner, source):
        return pl.ds(pl.multiple_of(owner * rows + source * cap, cap), cap)

    def pair_copy(d):
        to = e_peer(d)
        return remote(
            pairs.at[slot_rows(to, e)], wf.at[pl.ds(pl.multiple_of(e * cap, cap), cap)],
            a_send.at[d], a_recv.at[e], (p, to),
        )

    for d in range(1, n_e):
        pair_copy(d).start()
    wf[pl.ds(pl.multiple_of(e * cap, cap), cap), :] = pairs[slot_rows(e, e), :]

    sides = (e + 1 - 2 * (e % 2), lax.rem(e + 2, n_e))
    across = n_e - 1 - e

    def expert_rows(owner):
        return pl.ds(pl.multiple_of(owner * rows, rows), rows)

    def tangent_copy(zs, i):
        ref = tang.at[pl.ds(zs * CORES, CORES), mine]
        return remote(ref, ref, t_send.at[zs, i], t_recv.at[zs, i], (p, sides[i]))

    def tangent_arrival(zs, i):
        ref = tang.at[pl.ds(zs * CORES, CORES), expert_rows(sides[i])]
        return remote(ref, ref, t_send.at[zs, i], t_recv.at[zs, i], (p, sides[i]))

    def onward_copy(zs, i):
        ref = tang.at[zs * CORES + i, expert_rows(sides[i])]
        return remote(ref, ref, o_send.at[zs, i], o_recv.at[zs, i], (p, sides[1 - i]))

    def onward_arrival(zs, i):
        ref = tang.at[zs * CORES + i, expert_rows(across)]
        return remote(ref, ref, o_send.at[zs, i], o_recv.at[zs, i], (p, sides[1 - i]))

    def pass_on(zs):
        for i in range(2):
            tangent_arrival(zs, i).wait_recv()
            onward_copy(zs, i).start()

    def rows_out(zs):
        two = pl.ds(zs * CORES, CORES)
        return pltpu.make_async_copy(hall.at[two], hall_out.at[two], out_sem.at[0, zs])

    def tangents(zs):
        rows_out(zs).start()
        block = hall[pl.ds(zs * CORES, CORES)].reshape(CORES * rows, hall.shape[2])
        out = lax.dot_general(block, dirv[...], nt, preferred_element_type=jnp.float32)
        tang[pl.ds(zs * CORES, CORES), mine, :feat] = out.astype(jnp.bfloat16).reshape(CORES, rows, feat)
        for i in range(2):
            tangent_copy(zs, i).start()

    load_dir.wait()
    load_h.wait()
    sibling_copy(z, h_ref).wait_recv()
    tangents(z)

    def weight_copy(d):
        return remote(wall.at[p], wall.at[p], w_send.at[d], w_recv.at[z], (z_peer(d) * CORES + core, e))

    def weight_sibling(zs):
        ref = wall.at[zs * CORES + core]
        return remote(ref, ref, ws_send.at[zs], ws_recv.at[zs], (sib, e))

    def share_weights():
        for d in range(1, n_e):
            src = e_peer(d)
            remote(
                pairs.at[slot_rows(e, src)], wf.at[pl.ds(pl.multiple_of(src * cap, cap), cap)],
                a_send.at[d], a_recv.at[src], (p, src),
            ).wait_recv()
        weights = wf[...]
        high = weights.astype(jnp.bfloat16).astype(jnp.float32)
        wall[p] = (high + swap_blocks(weights - high, cap)).astype(jnp.bfloat16)
        for d in range(1, n_z):
            weight_copy(d).start()
        weight_sibling(z).start()

    def forward_weights(zs):
        ref = wall.at[zs * CORES + core]
        remote(ref, ref, w_send.at[1], w_recv.at[zs], (sib, e)).wait_recv()
        weight_sibling(zs).start()

    near = jnp.minimum(z, n_z - 1 - z)

    def source(j):
        if j == 0:
            return z
        s = (j + 1) // 2
        close = z - s if j % 2 else z + s
        far = jnp.where(2 * z < n_z - 1, j, n_z - 1 - j)
        return jnp.where(j <= 2 * near, close, far)

    def relay_copy(zs, c):
        to = jnp.where(zs < z, z + 1, z - 1)
        ref = hall.at[zs * CORES + core, pl.ds(c * part, part)]
        return remote(ref, ref, relay_send.at[zs, c], hz_recv.at[zs, c], (to * CORES + core, e))

    def relays(zs, fn):
        to = jnp.where(zs < z, z + 1, z - 1)
        pl.when((to >= 0) & (to < n_z))(fn)

    lane = lax.broadcasted_iota(jnp.int32, (rows, LANES), 1)
    row = lax.broadcasted_iota(jnp.int32, (rows, LANES), 0)
    direct = (lane // cap) % n_e == row // cap

    def adjoint_out(zs):
        two = pl.ds(zs * CORES, CORES)
        return pltpu.make_async_copy(adj.at[two], adj_out.at[two], out_sem.at[1, zs])

    def finish(zs):
        weight_sibling(zs).wait_recv()
        for i in range(2):
            onward_arrival(zs, i).wait_recv()
        for k in range(CORES):
            packed = wall[zs * CORES + k].astype(jnp.float32)
            high = jnp.where(direct, packed, 0.0)
            low = swap_blocks(packed - high, cap)
            both = jnp.concatenate([high, low], axis=0).astype(jnp.bfloat16)
            out = jnp.dot(both, tang[zs * CORES + k], preferred_element_type=jnp.float32)
            out = (out[:rows] + out[rows:]).astype(jnp.bfloat16)
            adj[zs * CORES + k] = out[:, :feat]
        adjoint_out(zs).start()

    for j in range(1, n_z):
        zs = source(j)
        for c in range(CHUNKS):
            relay_copy(zs, c).wait_recv()
            relays(zs, lambda zs=zs, c=c: relay_copy(zs, c).start())
        sibling_copy(zs, hall.at[zs * CORES + core]).start()
        if j == 1:
            share_weights()
        sibling_copy(zs, hall.at[zs * CORES + core]).wait_recv()
        tangents(zs)
        pass_on(source(j - 1))
        if j >= 2:
            forward_weights(source(j - 1))
            finish(source(j - 2))
    forward_weights(source(n_z - 1))
    finish(source(n_z - 2))
    pass_on(source(n_z - 1))
    finish(source(n_z - 1))

    for c in range(CHUNKS):
        for side in range(2):
            on_side(side, lambda side=side, c=c: own_copy(side, c).wait_send())
    for d in range(1, n_e):
        pair_copy(d).wait_send()
    for d in range(1, n_z):
        weight_copy(d).wait_send()
    for j in range(n_z):
        zs = source(j)
        adjoint_out(zs).wait()
        rows_out(zs).wait()
        sibling_copy(zs, hall.at[zs * CORES + core]).wait_send()
        weight_sibling(zs).wait_send()
        for i in range(2):
            tangent_copy(zs, i).wait_send()
            onward_copy(zs, i).wait_send()
        if j:
            for c in range(CHUNKS):
                relays(zs, lambda zs=zs, c=c: relay_copy(zs, c).wait_send())


def outer_kernel(adj_ref, rows_ref, out_ref, turned):
    @pl.when(pl.program_id(0) == 0)
    def _():
        turned[...] = adj_ref[...].T

    out_ref[0] = jnp.dot(turned[...], rows_ref[...], preferred_element_type=jnp.float32)


def body(cached_hidden, direction, expert_ids, gate_weights):
    n_dp, n_e = lax.axis_size("dp"), lax.axis_size("expert")
    rows, fw = cached_hidden.shape
    cap = rows // n_e
    feat = direction.shape[1]
    if n_e != 4 or n_e * rows != LANES or cap % 8 or rows % (16 * CHUNKS) or n_dp % CORES or n_dp < 2 * CORES:
        return general_body(cached_hidden, direction, expert_ids, gate_weights)
    n_z = n_dp // CORES
    wide = -(-feat // LANES) * LANES
    scale = 1.0 / math.sqrt(expert_ids.shape[0] * n_dp * n_e)
    hbm = pl.BlockSpec(memory_space=pltpu.HBM)
    dma = pltpu.SemaphoreType.DMA
    adjoint, rows_all = pl.pallas_call(
        functools.partial(kernel, n_dp, n_e, cap, scale),
        out_shape=(
            jax.ShapeDtypeStruct((n_dp, rows, feat), jnp.bfloat16),
            jax.ShapeDtypeStruct((n_dp, rows, fw), jnp.bfloat16),
        ),
        in_specs=[hbm] * 4,
        out_specs=(hbm, hbm),
        scratch_shapes=[
            pltpu.VMEM((n_dp, rows, feat), jnp.bfloat16),
            pltpu.VMEM((n_dp, rows, fw), jnp.bfloat16),
            pltpu.VMEM((feat, fw), jnp.bfloat16),
            pltpu.VMEM(expert_ids.shape[::-1], jnp.int32),
            pltpu.VMEM(gate_weights.shape[::-1], jnp.float32),
            pltpu.VMEM((n_dp, n_e * rows, wide), jnp.bfloat16),
            pltpu.VMEM((LANES, LANES), jnp.float32),
            pltpu.VMEM((rows, LANES), jnp.float32),
            pltpu.VMEM((n_dp, rows, LANES), jnp.bfloat16),
            dma((4,)),
            dma((2, n_z)),
            dma((2, CHUNKS)),
            dma((n_z, CHUNKS)),
            dma((n_z, CHUNKS)),
            dma((n_z,)),
            dma((n_z,)),
            dma((n_e,)),
            dma((n_e,)),
            dma((n_z,)),
            dma((n_z,)),
            dma((n_z,)),
            dma((n_z,)),
            dma((n_z, 2)),
            dma((n_z, 2)),
            dma((n_z, 2)),
            dma((n_z, 2)),
        ],
        compiler_params=pltpu.CompilerParams(
            collective_id=0, has_side_effects=True, vmem_limit_bytes=56 * 1024 * 1024
        ),
    )(cached_hidden, direction, expert_ids.T, gate_weights.T)
    tile = fw // 3 if fw % (3 * LANES) == 0 else fw
    return pl.pallas_call(
        outer_kernel,
        grid=(fw // tile,),
        out_shape=jax.ShapeDtypeStruct((1, feat, fw), jnp.float32),
        in_specs=[
            pl.BlockSpec((n_dp * rows, feat), lambda i: (0, 0)),
            pl.BlockSpec((n_dp * rows, tile), lambda i: (0, i)),
        ],
        out_specs=pl.BlockSpec((1, feat, tile), lambda i: (0, 0, i)),
        scratch_shapes=[pltpu.VMEM((feat, n_dp * rows), jnp.bfloat16)],
    )(adjoint.reshape(n_dp * rows, feat), rows_all.reshape(n_dp * rows, fw))


def solution(mesh):
    return jax.shard_map(
        body,
        mesh=mesh,
        in_specs=(
            P(("dp", "expert"), None),
            P("expert", "dp", None),
            P(("dp", "expert"), None),
            P(("dp", "expert"), None),
        ),
        out_specs=P("expert", "dp", None),
        check_vma=False,
    )
```

```python
import functools
import math

import jax
import jax.numpy as jnp
from jax import lax
from jax.experimental import pallas as pl
from jax.experimental.pallas import tpu as pltpu
from jax.sharding import PartitionSpec as P

MESH = pl.DeviceIdType.MESH
CORES = 2
LANES = 128
CHUNKS = 2


def slot_positions(block_ids, experts):
    flat = block_ids.reshape(-1)
    onehot = (flat[:, None] == jnp.arange(experts, dtype=jnp.int32)[None, :]).astype(jnp.int32)
    before = jnp.cumsum(onehot, axis=0) - onehot
    return jnp.sum(before * onehot, axis=1).reshape(block_ids.shape)


def general_body(cached_hidden, direction, expert_ids, gate_weights):
    dp_count = lax.axis_size("dp")
    owner_count = lax.axis_size("expert")
    slot_rows = cached_hidden.shape[0]
    capacity = slot_rows // owner_count
    tok_count = expert_ids.shape[0]
    width = direction.shape[1] * dp_count
    local_dir = direction[0]
    rows_all = lax.all_gather(cached_hidden, "dp", axis=0, tiled=True)
    tangent = lax.dot_general(
        rows_all, local_dir, (((1,), (1,)), ((), ())), preferred_element_type=jnp.float32
    )
    tangent = tangent.astype(jnp.bfloat16).reshape(
        dp_count, owner_count, capacity, local_dir.shape[0]
    )
    returned = lax.all_to_all(
        lax.all_to_all(tangent, "dp", split_axis=0, concat_axis=3, tiled=True),
        "expert",
        split_axis=1,
        concat_axis=1,
        tiled=True,
    )
    flat_rows = returned.reshape(owner_count * capacity, width)
    treated = expert_ids < owner_count
    slot_pos = slot_positions(expert_ids, owner_count)
    target = expert_ids * capacity + slot_pos
    lookup = jnp.where(treated, target, 0).reshape(-1)
    dropped = jnp.where(treated, target, owner_count * capacity).reshape(-1)
    gates = jnp.where(treated, gate_weights, 0.0)
    picked = jnp.take(flat_rows, lookup, axis=0).reshape(tok_count, expert_ids.shape[1], width)
    scale_factor = 1.0 / math.sqrt(tok_count * dp_count * owner_count)
    combined = jnp.sum(gates[..., None] * picked.astype(jnp.float32), axis=1) * scale_factor
    outgoing = (gates[..., None] * combined[:, None, :]).astype(jnp.bfloat16)
    buffer = jnp.zeros((owner_count * capacity, width), jnp.bfloat16)
    buffer = buffer.at[dropped].set(outgoing.reshape(-1, width), mode="drop")
    buffer = buffer.reshape(1, owner_count, capacity, width)
    arrived = lax.all_to_all(buffer, "expert", split_axis=1, concat_axis=1, tiled=True)
    adjoint = lax.all_to_all(arrived, "dp", split_axis=3, concat_axis=0, tiled=True)
    adjoint_rows = adjoint.reshape(-1, adjoint.shape[3])
    gradient = lax.dot_general(
        adjoint_rows, rows_all, (((0,), (0,)), ((), ())), preferred_element_type=jnp.float32
    )
    return gradient.reshape(1, gradient.shape[0], gradient.shape[1])


def swap_blocks(x, cap):
    lane = lax.broadcasted_iota(jnp.int32, x.shape, 1)
    back = pltpu.roll(x, LANES - cap, 1)
    ahead = pltpu.roll(x, cap, 1)
    return jnp.where((lane // cap) % 2 == 0, back, ahead)


def pair_matrix(ids, gates, q, n_e, cap, scale):
    topk, toks = ids.shape
    slot = lax.broadcasted_iota(jnp.int32, (LANES, toks), 0)
    slot_e, slot_q, slot_c = slot // (n_e * cap), (slot // cap) % n_e, slot % cap
    named = jnp.zeros((LANES, toks), jnp.float32)
    gate = jnp.zeros((LANES, toks), jnp.float32)
    for k in range(topk):
        same = ids[k : k + 1, :] == slot_e
        named = named + jnp.where(same, 1.0, 0.0)
        gate = gate + jnp.where(same, gates[k : k + 1, :], 0.0)
    row = lax.broadcasted_iota(jnp.int32, (toks, toks), 0)
    col = lax.broadcasted_iota(jnp.int32, (toks, toks), 1)
    earlier = jnp.where(row < col, 1.0, 0.0).astype(jnp.bfloat16)
    position = jnp.dot(named.astype(jnp.bfloat16), earlier, preferred_element_type=jnp.float32)
    held = (position == slot_c.astype(jnp.float32)) & (slot_q == q)
    slots = jnp.where(held, gate, 0.0)
    high = slots.astype(jnp.bfloat16)
    low = (slots - high.astype(jnp.float32)).astype(jnp.bfloat16)
    nt = (((1,), (1,)), ((), ()))
    total = lax.dot_general(high, high, nt, preferred_element_type=jnp.float32)
    total += lax.dot_general(high, low, nt, preferred_element_type=jnp.float32)
    total += lax.dot_general(low, high, nt, preferred_element_type=jnp.float32)
    return total * scale


def kernel(
    n_dp, n_e, cap, scale,
    h_ref, dir_ref, ids_ref, gates_ref,
    adj_out, hall_out,
    adj, hall, dirv, dirt, idv, gatev, tang, pairs, wf, wall,
    loc_sem, out_sem, own_send, relay_send, hz_recv, hs_send, hs_recv,
    a_send, a_recv, w_send, w_recv, ws_send, ws_recv, t_send, t_recv,
):
    n_z = n_dp // CORES
    rows = n_e * cap
    feat = dirv.shape[0]
    part = rows // CHUNKS
    p = lax.axis_index("dp")
    e = lax.axis_index("expert")
    z, core = p // CORES, p % CORES
    sib = z * CORES + (1 - core)

    load_dir = pltpu.make_async_copy(dir_ref.at[0], dirv, loc_sem.at[0])
    load_h = pltpu.make_async_copy(h_ref, hall.at[p], loc_sem.at[1])
    load_ids = pltpu.make_async_copy(ids_ref, idv, loc_sem.at[2])
    load_gates = pltpu.make_async_copy(gates_ref, gatev, loc_sem.at[3])
    load_ids.start()
    load_gates.start()
    load_h.start()
    load_dir.start()

    def z_peer(d):
        return lax.rem(z + d, n_z)

    def e_peer(d):
        return lax.rem(e + d, n_e)

    barrier = pltpu.get_barrier_semaphore()
    for d in range(1, n_z):
        pl.semaphore_signal(barrier, inc=1, device_id=(z_peer(d) * CORES + core, e), device_id_type=MESH)
    for d in range(1, n_e):
        pl.semaphore_signal(barrier, inc=1, device_id=(p, e_peer(d)), device_id_type=MESH)
    pl.semaphore_signal(barrier, inc=1, device_id=(sib, e), device_id_type=MESH)
    mine = pl.ds(pl.multiple_of(e * rows, rows), rows)
    tang[:, mine, feat // LANES * LANES :] = jnp.zeros(
        (n_dp, rows, tang.shape[2] - feat // LANES * LANES), jnp.bfloat16
    )
    pl.semaphore_wait(barrier, n_z + n_e - 1)

    def remote(src, dst, send, recv, dev):
        return pltpu.make_async_remote_copy(
            src_ref=src, dst_ref=dst, send_sem=send, recv_sem=recv, device_id=dev, device_id_type=MESH
        )

    def own_copy(side, c):
        to = z + 1 if side == 0 else z - 1
        return remote(
            h_ref.at[pl.ds(c * part, part)], hall.at[p, pl.ds(c * part, part)],
            own_send.at[side, c], hz_recv.at[z, c], (to * CORES + core, e),
        )

    def on_side(side, fn):
        pl.when(z + 1 < n_z if side == 0 else z > 0)(fn)

    for c in range(CHUNKS):
        for side in range(2):
            on_side(side, lambda side=side, c=c: own_copy(side, c).start())

    def sibling_copy(zs, src):
        row = zs * CORES + core
        return remote(src, hall.at[row], hs_send.at[zs], hs_recv.at[zs], (sib, e))

    sibling_copy(z, h_ref).start()

    load_ids.wait()
    load_gates.wait()
    pairs[...] = pair_matrix(idv[...], gatev[...], e, n_e, cap, scale)

    def slot_rows(owner, source):
        return pl.ds(pl.multiple_of(owner * rows + source * cap, cap), cap)

    def pair_copy(d):
        to = e_peer(d)
        return remote(
            pairs.at[slot_rows(to, e)], wf.at[pl.ds(pl.multiple_of(e * cap, cap), cap)],
            a_send.at[d], a_recv.at[e], (p, to),
        )

    for d in range(1, n_e):
        pair_copy(d).start()
    wf[pl.ds(pl.multiple_of(e * cap, cap), cap), :] = pairs[slot_rows(e, e), :]

    def tangent_copy(zs, d):
        ref = tang.at[pl.ds(zs * CORES, CORES), mine]
        return remote(ref, ref, t_send.at[zs, d], t_recv.at[zs, e], (p, e_peer(d)))

    def rows_out(zs):
        two = pl.ds(pl.multiple_of(zs * CORES * rows, CORES * rows), CORES * rows)
        src = hall.reshape(n_dp * rows, hall.shape[2])
        return pltpu.make_async_copy(src.at[two], hall_out.at[two], out_sem.at[0, zs])

    def tangents(zs):
        rows_out(zs).start()
        block = hall[pl.ds(zs * CORES, CORES)].reshape(CORES * rows, hall.shape[2])
        out = jnp.dot(block, dirt[...], preferred_element_type=jnp.float32)
        tang[pl.ds(zs * CORES, CORES), mine, :feat] = out.astype(jnp.bfloat16).reshape(CORES, rows, feat)
        for d in range(1, n_e):
            tangent_copy(zs, d).start()

    load_dir.wait()
    dirt[...] = dirv[...].T
    load_h.wait()
    sibling_copy(z, h_ref).wait_recv()
    tangents(z)

    def weight_copy(d):
        return remote(wall.at[p], wall.at[p], w_send.at[d], w_recv.at[z], (z_peer(d) * CORES + core, e))

    def weight_sibling(zs):
        ref = wall.at[zs * CORES + core]
        return remote(ref, ref, ws_send.at[zs], ws_recv.at[zs], (sib, e))

    def share_weights():
        for d in range(1, n_e):
            src = e_peer(d)
            remote(
                pairs.at[slot_rows(e, src)], wf.at[pl.ds(pl.multiple_of(src * cap, cap), cap)],
                a_send.at[d], a_recv.at[src], (p, src),
            ).wait_recv()
        weights = wf[...]
        high = weights.astype(jnp.bfloat16).astype(jnp.float32)
        wall[p] = (high + swap_blocks(weights - high, cap)).astype(jnp.bfloat16)
        for d in range(1, n_z):
            weight_copy(d).start()
        weight_sibling(z).start()

    def forward_weights(zs):
        ref = wall.at[zs * CORES + core]
        remote(ref, ref, w_send.at[1], w_recv.at[zs], (sib, e)).wait_recv()
        weight_sibling(zs).start()

    near = jnp.minimum(z, n_z - 1 - z)

    def source(j):
        if j == 0:
            return z
        s = (j + 1) // 2
        close = z - s if j % 2 else z + s
        far = jnp.where(2 * z < n_z - 1, j, n_z - 1 - j)
        return jnp.where(j <= 2 * near, close, far)

    def relay_copy(zs, c):
        to = jnp.where(zs < z, z + 1, z - 1)
        ref = hall.at[zs * CORES + core, pl.ds(c * part, part)]
        return remote(ref, ref, relay_send.at[zs, c], hz_recv.at[zs, c], (to * CORES + core, e))

    def relays(zs, fn):
        to = jnp.where(zs < z, z + 1, z - 1)
        pl.when((to >= 0) & (to < n_z))(fn)

    lane = lax.broadcasted_iota(jnp.int32, (rows, LANES), 1)
    row = lax.broadcasted_iota(jnp.int32, (rows, LANES), 0)
    direct = (lane // cap) % n_e == row // cap

    def adjoint_out(zs):
        two = pl.ds(pl.multiple_of(zs * CORES * rows, CORES * rows), CORES * rows)
        return pltpu.make_async_copy(adj.at[two], adj_out.at[two], out_sem.at[1, zs])

    def finish(zs):
        weight_sibling(zs).wait_recv()
        for d in range(1, n_e):
            src = e_peer(d)
            ref = tang.at[pl.ds(zs * CORES, CORES), pl.ds(pl.multiple_of(src * rows, rows), rows)]
            remote(ref, ref, t_send.at[zs, d], t_recv.at[zs, src], (p, src)).wait_recv()
        for k in range(CORES):
            packed = wall[zs * CORES + k].astype(jnp.float32)
            high = jnp.where(direct, packed, 0.0)
            low = swap_blocks(packed - high, cap)
            both = jnp.concatenate([high, low], axis=0).astype(jnp.bfloat16)
            out = jnp.dot(both, tang[zs * CORES + k], preferred_element_type=jnp.float32)
            out = (out[:rows] + out[rows:]).astype(jnp.bfloat16)
            adj[pl.ds(pl.multiple_of((zs * CORES + k) * rows, rows), rows), :] = out[:, :feat]
        adjoint_out(zs).start()

    for j in range(1, n_z):
        zs = source(j)
        for c in range(CHUNKS):
            relay_copy(zs, c).wait_recv()
            relays(zs, lambda zs=zs, c=c: relay_copy(zs, c).start())
        sibling_copy(zs, hall.at[zs * CORES + core]).start()
        if j == 1:
            share_weights()
        if j >= 2:
            forward_weights(source(j - 1))
            finish(source(j - 2))
        sibling_copy(zs, hall.at[zs * CORES + core]).wait_recv()
        tangents(zs)
    forward_weights(source(n_z - 1))
    finish(source(n_z - 2))
    finish(source(n_z - 1))

    for c in range(CHUNKS):
        for side in range(2):
            on_side(side, lambda side=side, c=c: own_copy(side, c).wait_send())
    for d in range(1, n_e):
        pair_copy(d).wait_send()
    for d in range(1, n_z):
        weight_copy(d).wait_send()
    for j in range(n_z):
        zs = source(j)
        adjoint_out(zs).wait()
        rows_out(zs).wait()
        sibling_copy(zs, hall.at[zs * CORES + core]).wait_send()
        weight_sibling(zs).wait_send()
        for d in range(1, n_e):
            tangent_copy(zs, d).wait_send()
        if j:
            for c in range(CHUNKS):
                relays(zs, lambda zs=zs, c=c: relay_copy(zs, c).wait_send())


def body(cached_hidden, direction, expert_ids, gate_weights):
    n_dp, n_e = lax.axis_size("dp"), lax.axis_size("expert")
    rows, fw = cached_hidden.shape
    cap = rows // n_e
    feat = direction.shape[1]
    if n_e * rows != LANES or cap % 8 or rows % (16 * CHUNKS) or n_dp % CORES or n_dp < 2 * CORES:
        return general_body(cached_hidden, direction, expert_ids, gate_weights)
    n_z = n_dp // CORES
    wide = -(-feat // LANES) * LANES
    scale = 1.0 / math.sqrt(expert_ids.shape[0] * n_dp * n_e)
    hbm = pl.BlockSpec(memory_space=pltpu.HBM)
    dma = pltpu.SemaphoreType.DMA
    adjoint, rows_all = pl.pallas_call(
        functools.partial(kernel, n_dp, n_e, cap, scale),
        out_shape=(
            jax.ShapeDtypeStruct((n_dp * rows, feat), jnp.bfloat16),
            jax.ShapeDtypeStruct((n_dp * rows, fw), jnp.bfloat16),
        ),
        in_specs=[hbm] * 4,
        out_specs=(hbm, hbm),
        scratch_shapes=[
            pltpu.VMEM((n_dp * rows, feat), jnp.bfloat16),
            pltpu.VMEM((n_dp, rows, fw), jnp.bfloat16),
            pltpu.VMEM((feat, fw), jnp.bfloat16),
            pltpu.VMEM((fw, feat), jnp.bfloat16),
            pltpu.VMEM(expert_ids.shape[::-1], jnp.int32),
            pltpu.VMEM(gate_weights.shape[::-1], jnp.float32),
            pltpu.VMEM((n_dp, n_e * rows, wide), jnp.bfloat16),
            pltpu.VMEM((LANES, LANES), jnp.float32),
            pltpu.VMEM((rows, LANES), jnp.float32),
            pltpu.VMEM((n_dp, rows, LANES), jnp.bfloat16),
            dma((4,)),
            dma((2, n_z)),
            dma((2, CHUNKS)),
            dma((n_z, CHUNKS)),
            dma((n_z, CHUNKS)),
            dma((n_z,)),
            dma((n_z,)),
            dma((n_e,)),
            dma((n_e,)),
            dma((n_z,)),
            dma((n_z,)),
            dma((n_z,)),
            dma((n_z,)),
            dma((n_z, n_e)),
            dma((n_z, n_e)),
        ],
        compiler_params=pltpu.CompilerParams(
            collective_id=0, has_side_effects=True, vmem_limit_bytes=56 * 1024 * 1024
        ),
    )(cached_hidden, direction, expert_ids.T, gate_weights.T)
    gradient = lax.dot_general(
        adjoint,
        rows_all,
        (((0,), (0,)), ((), ())),
        preferred_element_type=jnp.float32,
    )
    return gradient.reshape(1, feat, fw)


def solution(mesh):
    return jax.shard_map(
        body,
        mesh=mesh,
        in_specs=(
            P(("dp", "expert"), None),
            P("expert", "dp", None),
            P(("dp", "expert"), None),
            P(("dp", "expert"), None),
        ),
        out_specs=P("expert", "dp", None),
        check_vma=False,
    )
```

```python
import functools
import math

import jax
import jax.numpy as jnp
from jax import lax
from jax.experimental import pallas as pl
from jax.experimental.pallas import tpu as pltpu
from jax.sharding import PartitionSpec as P

MESH = pl.DeviceIdType.MESH
CORES = 2
LANES = 128
CHUNKS = 2


def slot_positions(block_ids, experts):
    flat = block_ids.reshape(-1)
    onehot = (flat[:, None] == jnp.arange(experts, dtype=jnp.int32)[None, :]).astype(jnp.int32)
    before = jnp.cumsum(onehot, axis=0) - onehot
    return jnp.sum(before * onehot, axis=1).reshape(block_ids.shape)


def general_body(cached_hidden, direction, expert_ids, gate_weights):
    dp_count = lax.axis_size("dp")
    owner_count = lax.axis_size("expert")
    slot_rows = cached_hidden.shape[0]
    capacity = slot_rows // owner_count
    tok_count = expert_ids.shape[0]
    width = direction.shape[1] * dp_count
    local_dir = direction[0]
    rows_all = lax.all_gather(cached_hidden, "dp", axis=0, tiled=True)
    tangent = lax.dot_general(
        rows_all, local_dir, (((1,), (1,)), ((), ())), preferred_element_type=jnp.float32
    )
    tangent = tangent.astype(jnp.bfloat16).reshape(
        dp_count, owner_count, capacity, local_dir.shape[0]
    )
    returned = lax.all_to_all(
        lax.all_to_all(tangent, "dp", split_axis=0, concat_axis=3, tiled=True),
        "expert",
        split_axis=1,
        concat_axis=1,
        tiled=True,
    )
    flat_rows = returned.reshape(owner_count * capacity, width)
    treated = expert_ids < owner_count
    slot_pos = slot_positions(expert_ids, owner_count)
    target = expert_ids * capacity + slot_pos
    lookup = jnp.where(treated, target, 0).reshape(-1)
    dropped = jnp.where(treated, target, owner_count * capacity).reshape(-1)
    gates = jnp.where(treated, gate_weights, 0.0)
    picked = jnp.take(flat_rows, lookup, axis=0).reshape(tok_count, expert_ids.shape[1], width)
    scale_factor = 1.0 / math.sqrt(tok_count * dp_count * owner_count)
    combined = jnp.sum(gates[..., None] * picked.astype(jnp.float32), axis=1) * scale_factor
    outgoing = (gates[..., None] * combined[:, None, :]).astype(jnp.bfloat16)
    buffer = jnp.zeros((owner_count * capacity, width), jnp.bfloat16)
    buffer = buffer.at[dropped].set(outgoing.reshape(-1, width), mode="drop")
    buffer = buffer.reshape(1, owner_count, capacity, width)
    arrived = lax.all_to_all(buffer, "expert", split_axis=1, concat_axis=1, tiled=True)
    adjoint = lax.all_to_all(arrived, "dp", split_axis=3, concat_axis=0, tiled=True)
    adjoint_rows = adjoint.reshape(-1, adjoint.shape[3])
    gradient = lax.dot_general(
        adjoint_rows, rows_all, (((0,), (0,)), ((), ())), preferred_element_type=jnp.float32
    )
    return gradient.reshape(1, gradient.shape[0], gradient.shape[1])


def swap_blocks(x, cap):
    lane = lax.broadcasted_iota(jnp.int32, x.shape, 1)
    back = pltpu.roll(x, LANES - cap, 1)
    ahead = pltpu.roll(x, cap, 1)
    return jnp.where((lane // cap) % 2 == 0, back, ahead)


def pair_matrix(ids, gates, q, n_e, cap, scale):
    topk, toks = ids.shape
    slot = lax.broadcasted_iota(jnp.int32, (LANES, toks), 0)
    slot_e, slot_q, slot_c = slot // (n_e * cap), (slot // cap) % n_e, slot % cap
    named = jnp.zeros((LANES, toks), jnp.float32)
    gate = jnp.zeros((LANES, toks), jnp.float32)
    for k in range(topk):
        same = ids[k : k + 1, :] == slot_e
        named = named + jnp.where(same, 1.0, 0.0)
        gate = gate + jnp.where(same, gates[k : k + 1, :], 0.0)
    row = lax.broadcasted_iota(jnp.int32, (toks, toks), 0)
    col = lax.broadcasted_iota(jnp.int32, (toks, toks), 1)
    earlier = jnp.where(row < col, 1.0, 0.0).astype(jnp.bfloat16)
    position = jnp.dot(named.astype(jnp.bfloat16), earlier, preferred_element_type=jnp.float32)
    held = (position == slot_c.astype(jnp.float32)) & (slot_q == q)
    slots = jnp.where(held, gate, 0.0)
    high = slots.astype(jnp.bfloat16)
    low = (slots - high.astype(jnp.float32)).astype(jnp.bfloat16)
    nt = (((1,), (1,)), ((), ()))
    total = lax.dot_general(high, high, nt, preferred_element_type=jnp.float32)
    total += lax.dot_general(high, low, nt, preferred_element_type=jnp.float32)
    total += lax.dot_general(low, high, nt, preferred_element_type=jnp.float32)
    return total * scale


def kernel(
    n_dp, n_e, cap, scale,
    h_ref, dir_ref, ids_ref, gates_ref,
    adj_out, hall_out,
    adj, hall, dirv, dirt, idv, gatev, tang, pairs, wf, wall,
    loc_sem, out_sem, own_send, relay_send, hz_recv, hs_send, hs_recv,
    a_send, a_recv, w_send, wr_send, w_recv, ws_send, ws_recv, t_send, t_recv,
):
    n_z = n_dp // CORES
    rows = n_e * cap
    feat = dirv.shape[0]
    part = rows // CHUNKS
    p = lax.axis_index("dp")
    e = lax.axis_index("expert")
    z, core = p // CORES, p % CORES
    sib = z * CORES + (1 - core)

    load_dir = pltpu.make_async_copy(dir_ref.at[0], dirv, loc_sem.at[0])
    load_h = pltpu.make_async_copy(h_ref, hall.at[p], loc_sem.at[1])
    load_ids = pltpu.make_async_copy(ids_ref, idv, loc_sem.at[2])
    load_gates = pltpu.make_async_copy(gates_ref, gatev, loc_sem.at[3])
    load_ids.start()
    load_gates.start()
    load_h.start()
    load_dir.start()

    def on_side(side, fn):
        pl.when(z + 1 < n_z if side == 0 else z > 0)(fn)

    def e_peer(d):
        return lax.rem(e + d, n_e)

    barrier = pltpu.get_barrier_semaphore()
    for side in range(2):
        to = (z + 1 if side == 0 else z - 1) * CORES + core
        on_side(
            side,
            lambda to=to: pl.semaphore_signal(barrier, inc=1, device_id=(to, e), device_id_type=MESH),
        )
    for d in range(1, n_e):
        pl.semaphore_signal(barrier, inc=1, device_id=(p, e_peer(d)), device_id_type=MESH)
    pl.semaphore_signal(barrier, inc=1, device_id=(sib, e), device_id_type=MESH)
    mine = pl.ds(pl.multiple_of(e * rows, rows), rows)
    tang[:, mine, feat // LANES * LANES :] = jnp.zeros(
        (n_dp, rows, tang.shape[2] - feat // LANES * LANES), jnp.bfloat16
    )
    on_line = jnp.where(z > 0, 1, 0) + jnp.where(z + 1 < n_z, 1, 0)
    pl.semaphore_wait(barrier, on_line + n_e)

    def remote(src, dst, send, recv, dev):
        return pltpu.make_async_remote_copy(
            src_ref=src, dst_ref=dst, send_sem=send, recv_sem=recv, device_id=dev, device_id_type=MESH
        )

    def own_copy(side, c):
        to = z + 1 if side == 0 else z - 1
        return remote(
            h_ref.at[pl.ds(c * part, part)], hall.at[p, pl.ds(c * part, part)],
            own_send.at[side, c], hz_recv.at[z, c], (to * CORES + core, e),
        )

    for c in range(CHUNKS):
        for side in range(2):
            on_side(side, lambda side=side, c=c: own_copy(side, c).start())

    def sibling_copy(zs, src):
        row = zs * CORES + core
        return remote(src, hall.at[row], hs_send.at[zs], hs_recv.at[zs], (sib, e))

    sibling_copy(z, h_ref).start()

    load_ids.wait()
    load_gates.wait()
    pairs[...] = pair_matrix(idv[...], gatev[...], e, n_e, cap, scale)

    def slot_rows(owner, source):
        return pl.ds(pl.multiple_of(owner * rows + source * cap, cap), cap)

    def pair_copy(d):
        to = e_peer(d)
        return remote(
            pairs.at[slot_rows(to, e)], wf.at[pl.ds(pl.multiple_of(e * cap, cap), cap)],
            a_send.at[d], a_recv.at[e], (p, to),
        )

    for d in range(1, n_e):
        pair_copy(d).start()
    wf[pl.ds(pl.multiple_of(e * cap, cap), cap), :] = pairs[slot_rows(e, e), :]

    def tangent_copy(zs, d):
        ref = tang.at[pl.ds(zs * CORES, CORES), mine]
        return remote(ref, ref, t_send.at[zs, d], t_recv.at[zs, e], (p, e_peer(d)))

    def rows_out(zs):
        two = pl.ds(pl.multiple_of(zs * CORES * rows, CORES * rows), CORES * rows)
        src = hall.reshape(n_dp * rows, hall.shape[2])
        return pltpu.make_async_copy(src.at[two], hall_out.at[two], out_sem.at[0, zs])

    def tangents(zs):
        rows_out(zs).start()
        block = hall[pl.ds(zs * CORES, CORES)].reshape(CORES * rows, hall.shape[2])
        out = jnp.dot(block, dirt[...], preferred_element_type=jnp.float32)
        tang[pl.ds(zs * CORES, CORES), mine, :feat] = out.astype(jnp.bfloat16).reshape(CORES, rows, feat)
        for d in range(1, n_e):
            tangent_copy(zs, d).start()

    load_dir.wait()
    dirt[...] = dirv[...].T
    load_h.wait()
    sibling_copy(z, h_ref).wait_recv()
    tangents(z)

    def weight_copy(side):
        to = z + 1 if side == 0 else z - 1
        return remote(wall.at[p], wall.at[p], w_send.at[side], w_recv.at[z], (to * CORES + core, e))

    def weight_relay(zs):
        to = jnp.where(zs < z, z + 1, z - 1)
        ref = wall.at[zs * CORES + core]
        return remote(ref, ref, wr_send.at[zs], w_recv.at[zs], (to * CORES + core, e))

    def weight_sibling(zs):
        ref = wall.at[zs * CORES + core]
        return remote(ref, ref, ws_send.at[zs], ws_recv.at[zs], (sib, e))

    def share_weights():
        for d in range(1, n_e):
            src = e_peer(d)
            remote(
                pairs.at[slot_rows(e, src)], wf.at[pl.ds(pl.multiple_of(src * cap, cap), cap)],
                a_send.at[d], a_recv.at[src], (p, src),
            ).wait_recv()
        weights = wf[...]
        high = weights.astype(jnp.bfloat16).astype(jnp.float32)
        wall[p] = (high + swap_blocks(weights - high, cap)).astype(jnp.bfloat16)
        for side in range(2):
            on_side(side, lambda side=side: weight_copy(side).start())
        weight_sibling(z).start()

    def forward_weights(zs):
        weight_relay(zs).wait_recv()
        relays(zs, lambda: weight_relay(zs).start())
        weight_sibling(zs).start()

    near = jnp.minimum(z, n_z - 1 - z)

    def source(j):
        if j == 0:
            return z
        s = (j + 1) // 2
        close = z - s if j % 2 else z + s
        far = jnp.where(2 * z < n_z - 1, j, n_z - 1 - j)
        return jnp.where(j <= 2 * near, close, far)

    def relay_copy(zs, c):
        to = jnp.where(zs < z, z + 1, z - 1)
        ref = hall.at[zs * CORES + core, pl.ds(c * part, part)]
        return remote(ref, ref, relay_send.at[zs, c], hz_recv.at[zs, c], (to * CORES + core, e))

    def relays(zs, fn):
        to = jnp.where(zs < z, z + 1, z - 1)
        pl.when((to >= 0) & (to < n_z))(fn)

    lane = lax.broadcasted_iota(jnp.int32, (rows, LANES), 1)
    row = lax.broadcasted_iota(jnp.int32, (rows, LANES), 0)
    direct = (lane // cap) % n_e == row // cap

    def adjoint_out(zs):
        two = pl.ds(pl.multiple_of(zs * CORES * rows, CORES * rows), CORES * rows)
        return pltpu.make_async_copy(adj.at[two], adj_out.at[two], out_sem.at[1, zs])

    def finish(zs):
        weight_sibling(zs).wait_recv()
        for d in range(1, n_e):
            src = e_peer(d)
            ref = tang.at[pl.ds(zs * CORES, CORES), pl.ds(pl.multiple_of(src * rows, rows), rows)]
            remote(ref, ref, t_send.at[zs, d], t_recv.at[zs, src], (p, src)).wait_recv()
        for k in range(CORES):
            packed = wall[zs * CORES + k].astype(jnp.float32)
            high = jnp.where(direct, packed, 0.0)
            low = swap_blocks(packed - high, cap)
            both = jnp.concatenate([high, low], axis=0).astype(jnp.bfloat16)
            out = jnp.dot(both, tang[zs * CORES + k], preferred_element_type=jnp.float32)
            out = (out[:rows] + out[rows:]).astype(jnp.bfloat16)
            adj[pl.ds(pl.multiple_of((zs * CORES + k) * rows, rows), rows), :] = out[:, :feat]
        adjoint_out(zs).start()

    for j in range(1, n_z):
        zs = source(j)
        for c in range(CHUNKS):
            relay_copy(zs, c).wait_recv()
            relays(zs, lambda zs=zs, c=c: relay_copy(zs, c).start())
        sibling_copy(zs, hall.at[zs * CORES + core]).start()
        if j == 1:
            share_weights()
        if j >= 2:
            forward_weights(source(j - 1))
            finish(source(j - 2))
        sibling_copy(zs, hall.at[zs * CORES + core]).wait_recv()
        tangents(zs)
    forward_weights(source(n_z - 1))
    finish(source(n_z - 2))
    finish(source(n_z - 1))

    for c in range(CHUNKS):
        for side in range(2):
            on_side(side, lambda side=side, c=c: own_copy(side, c).wait_send())
    for d in range(1, n_e):
        pair_copy(d).wait_send()
    for side in range(2):
        on_side(side, lambda side=side: weight_copy(side).wait_send())
    for j in range(n_z):
        zs = source(j)
        adjoint_out(zs).wait()
        rows_out(zs).wait()
        sibling_copy(zs, hall.at[zs * CORES + core]).wait_send()
        weight_sibling(zs).wait_send()
        for d in range(1, n_e):
            tangent_copy(zs, d).wait_send()
        if j:
            for c in range(CHUNKS):
                relays(zs, lambda zs=zs, c=c: relay_copy(zs, c).wait_send())
            relays(zs, lambda zs=zs: weight_relay(zs).wait_send())


def body(cached_hidden, direction, expert_ids, gate_weights):
    n_dp, n_e = lax.axis_size("dp"), lax.axis_size("expert")
    rows, fw = cached_hidden.shape
    cap = rows // n_e
    feat = direction.shape[1]
    if n_e * rows != LANES or cap % 8 or rows % (16 * CHUNKS) or n_dp % CORES or n_dp < 2 * CORES:
        return general_body(cached_hidden, direction, expert_ids, gate_weights)
    n_z = n_dp // CORES
    wide = -(-feat // LANES) * LANES
    scale = 1.0 / math.sqrt(expert_ids.shape[0] * n_dp * n_e)
    hbm = pl.BlockSpec(memory_space=pltpu.HBM)
    dma = pltpu.SemaphoreType.DMA
    adjoint, rows_all = pl.pallas_call(
        functools.partial(kernel, n_dp, n_e, cap, scale),
        out_shape=(
            jax.ShapeDtypeStruct((n_dp * rows, feat), jnp.bfloat16),
            jax.ShapeDtypeStruct((n_dp * rows, fw), jnp.bfloat16),
        ),
        in_specs=[hbm] * 4,
        out_specs=(hbm, hbm),
        scratch_shapes=[
            pltpu.VMEM((n_dp * rows, feat), jnp.bfloat16),
            pltpu.VMEM((n_dp, rows, fw), jnp.bfloat16),
            pltpu.VMEM((feat, fw), jnp.bfloat16),
            pltpu.VMEM((fw, feat), jnp.bfloat16),
            pltpu.VMEM(expert_ids.shape[::-1], jnp.int32),
            pltpu.VMEM(gate_weights.shape[::-1], jnp.float32),
            pltpu.VMEM((n_dp, n_e * rows, wide), jnp.bfloat16),
            pltpu.VMEM((LANES, LANES), jnp.float32),
            pltpu.VMEM((rows, LANES), jnp.float32),
            pltpu.VMEM((n_dp, rows, LANES), jnp.bfloat16),
            dma((4,)),
            dma((2, n_z)),
            dma((2, CHUNKS)),
            dma((n_z, CHUNKS)),
            dma((n_z, CHUNKS)),
            dma((n_z,)),
            dma((n_z,)),
            dma((n_e,)),
            dma((n_e,)),
            dma((2,)),
            dma((n_z,)),
            dma((n_z,)),
            dma((n_z,)),
            dma((n_z,)),
            dma((n_z, n_e)),
            dma((n_z, n_e)),
        ],
        compiler_params=pltpu.CompilerParams(
            collective_id=0, has_side_effects=True, vmem_limit_bytes=56 * 1024 * 1024
        ),
    )(cached_hidden, direction, expert_ids.T, gate_weights.T)
    gradient = lax.dot_general(
        adjoint,
        rows_all,
        (((0,), (0,)), ((), ())),
        preferred_element_type=jnp.float32,
    )
    return gradient.reshape(1, feat, fw)


def solution(mesh):
    return jax.shard_map(
        body,
        mesh=mesh,
        in_specs=(
            P(("dp", "expert"), None),
            P("expert", "dp", None),
            P(("dp", "expert"), None),
            P(("dp", "expert"), None),
        ),
        out_specs=P("expert", "dp", None),
        check_vma=False,
    )
```

```python
import functools
import math

import jax
import jax.numpy as jnp
from jax import lax
from jax.experimental import pallas as pl
from jax.experimental.pallas import tpu as pltpu
from jax.sharding import PartitionSpec as P

MESH = pl.DeviceIdType.MESH
CORES = 2
LANES = 128
CHUNKS = 2


def slot_positions(block_ids, experts):
    flat = block_ids.reshape(-1)
    onehot = (flat[:, None] == jnp.arange(experts, dtype=jnp.int32)[None, :]).astype(jnp.int32)
    before = jnp.cumsum(onehot, axis=0) - onehot
    return jnp.sum(before * onehot, axis=1).reshape(block_ids.shape)


def general_body(cached_hidden, direction, expert_ids, gate_weights):
    dp_count = lax.axis_size("dp")
    owner_count = lax.axis_size("expert")
    slot_rows = cached_hidden.shape[0]
    capacity = slot_rows // owner_count
    tok_count = expert_ids.shape[0]
    width = direction.shape[1] * dp_count
    local_dir = direction[0]
    rows_all = lax.all_gather(cached_hidden, "dp", axis=0, tiled=True)
    tangent = lax.dot_general(
        rows_all, local_dir, (((1,), (1,)), ((), ())), preferred_element_type=jnp.float32
    )
    tangent = tangent.astype(jnp.bfloat16).reshape(
        dp_count, owner_count, capacity, local_dir.shape[0]
    )
    returned = lax.all_to_all(
        lax.all_to_all(tangent, "dp", split_axis=0, concat_axis=3, tiled=True),
        "expert",
        split_axis=1,
        concat_axis=1,
        tiled=True,
    )
    flat_rows = returned.reshape(owner_count * capacity, width)
    treated = expert_ids < owner_count
    slot_pos = slot_positions(expert_ids, owner_count)
    target = expert_ids * capacity + slot_pos
    lookup = jnp.where(treated, target, 0).reshape(-1)
    dropped = jnp.where(treated, target, owner_count * capacity).reshape(-1)
    gates = jnp.where(treated, gate_weights, 0.0)
    picked = jnp.take(flat_rows, lookup, axis=0).reshape(tok_count, expert_ids.shape[1], width)
    scale_factor = 1.0 / math.sqrt(tok_count * dp_count * owner_count)
    combined = jnp.sum(gates[..., None] * picked.astype(jnp.float32), axis=1) * scale_factor
    outgoing = (gates[..., None] * combined[:, None, :]).astype(jnp.bfloat16)
    buffer = jnp.zeros((owner_count * capacity, width), jnp.bfloat16)
    buffer = buffer.at[dropped].set(outgoing.reshape(-1, width), mode="drop")
    buffer = buffer.reshape(1, owner_count, capacity, width)
    arrived = lax.all_to_all(buffer, "expert", split_axis=1, concat_axis=1, tiled=True)
    adjoint = lax.all_to_all(arrived, "dp", split_axis=3, concat_axis=0, tiled=True)
    adjoint_rows = adjoint.reshape(-1, adjoint.shape[3])
    gradient = lax.dot_general(
        adjoint_rows, rows_all, (((0,), (0,)), ((), ())), preferred_element_type=jnp.float32
    )
    return gradient.reshape(1, gradient.shape[0], gradient.shape[1])


def swap_blocks(x, cap):
    lane = lax.broadcasted_iota(jnp.int32, x.shape, 1)
    back = pltpu.roll(x, LANES - cap, 1)
    ahead = pltpu.roll(x, cap, 1)
    return jnp.where((lane // cap) % 2 == 0, back, ahead)


def pair_matrix(ids, gates, q, n_e, cap, scale):
    topk, toks = ids.shape
    slot = lax.broadcasted_iota(jnp.int32, (LANES, toks), 0)
    slot_e, slot_q, slot_c = slot // (n_e * cap), (slot // cap) % n_e, slot % cap
    named = jnp.zeros((LANES, toks), jnp.float32)
    gate = jnp.zeros((LANES, toks), jnp.float32)
    for k in range(topk):
        same = ids[k : k + 1, :] == slot_e
        named = named + jnp.where(same, 1.0, 0.0)
        gate = gate + jnp.where(same, gates[k : k + 1, :], 0.0)
    row = lax.broadcasted_iota(jnp.int32, (toks, toks), 0)
    col = lax.broadcasted_iota(jnp.int32, (toks, toks), 1)
    earlier = jnp.where(row < col, 1.0, 0.0).astype(jnp.bfloat16)
    position = jnp.dot(named.astype(jnp.bfloat16), earlier, preferred_element_type=jnp.float32)
    held = (position == slot_c.astype(jnp.float32)) & (slot_q == q)
    slots = jnp.where(held, gate, 0.0)
    high = slots.astype(jnp.bfloat16)
    low = (slots - high.astype(jnp.float32)).astype(jnp.bfloat16)
    nt = (((1,), (1,)), ((), ()))
    total = lax.dot_general(high, high, nt, preferred_element_type=jnp.float32)
    total += lax.dot_general(high, low, nt, preferred_element_type=jnp.float32)
    total += lax.dot_general(low, high, nt, preferred_element_type=jnp.float32)
    return total * scale


def kernel(
    n_dp, n_e, cap, scale,
    h_ref, dir_ref, ids_ref, gates_ref,
    adj_out, hall_out,
    adj, hall, dirv, dirt, idv, gatev, tang, pairs, wf, wall,
    loc_sem, out_sem, own_send, relay_send, hz_recv, hs_send, hs_recv,
    a_send, a_recv, w_send, wr_send, w_recv, ws_send, ws_recv, t_send, t_recv,
):
    n_z = n_dp // CORES
    rows = n_e * cap
    feat = dirv.shape[0]
    part = rows // CHUNKS
    p = lax.axis_index("dp")
    e = lax.axis_index("expert")
    z, core = p // CORES, p % CORES
    sib = z * CORES + (1 - core)

    load_dir = pltpu.make_async_copy(dir_ref.at[0], dirv, loc_sem.at[0])
    load_h = pltpu.make_async_copy(h_ref, hall.at[p], loc_sem.at[1])
    load_ids = pltpu.make_async_copy(ids_ref, idv, loc_sem.at[2])
    load_gates = pltpu.make_async_copy(gates_ref, gatev, loc_sem.at[3])
    load_ids.start()
    load_gates.start()
    load_h.start()
    load_dir.start()

    def on_side(side, fn):
        pl.when(z + 1 < n_z if side == 0 else z > 0)(fn)

    def e_peer(d):
        return lax.rem(e + d, n_e)

    barrier = pltpu.get_barrier_semaphore()
    for side in range(2):
        to = (z + 1 if side == 0 else z - 1) * CORES + core
        on_side(
            side,
            lambda to=to: pl.semaphore_signal(barrier, inc=1, device_id=(to, e), device_id_type=MESH),
        )
    for d in range(1, n_e):
        pl.semaphore_signal(barrier, inc=1, device_id=(p, e_peer(d)), device_id_type=MESH)
    pl.semaphore_signal(barrier, inc=1, device_id=(sib, e), device_id_type=MESH)
    mine = pl.ds(pl.multiple_of(e * rows, rows), rows)
    tang[:, mine, feat // LANES * LANES :] = jnp.zeros(
        (n_dp, rows, tang.shape[2] - feat // LANES * LANES), jnp.bfloat16
    )
    on_line = jnp.where(z > 0, 1, 0) + jnp.where(z + 1 < n_z, 1, 0)
    pl.semaphore_wait(barrier, on_line + n_e)

    def remote(src, dst, send, recv, dev):
        return pltpu.make_async_remote_copy(
            src_ref=src, dst_ref=dst, send_sem=send, recv_sem=recv, device_id=dev, device_id_type=MESH
        )

    def own_copy(side, c):
        to = z + 1 if side == 0 else z - 1
        return remote(
            h_ref.at[pl.ds(c * part, part)], hall.at[p, pl.ds(c * part, part)],
            own_send.at[side, c], hz_recv.at[z, c], (to * CORES + core, e),
        )

    for c in range(CHUNKS):
        for side in range(2):
            on_side(side, lambda side=side, c=c: own_copy(side, c).start())

    def sibling_copy(zs, src):
        row = zs * CORES + core
        return remote(src, hall.at[row], hs_send.at[zs], hs_recv.at[zs], (sib, e))

    sibling_copy(z, h_ref).start()

    load_ids.wait()
    load_gates.wait()
    pairs[...] = pair_matrix(idv[...], gatev[...], e, n_e, cap, scale)

    def slot_rows(owner, source):
        return pl.ds(pl.multiple_of(owner * rows + source * cap, cap), cap)

    def pair_copy(d):
        to = e_peer(d)
        return remote(
            pairs.at[slot_rows(to, e)], wf.at[pl.ds(pl.multiple_of(e * cap, cap), cap)],
            a_send.at[d], a_recv.at[e], (p, to),
        )

    for d in range(1, n_e):
        pair_copy(d).start()
    wf[pl.ds(pl.multiple_of(e * cap, cap), cap), :] = pairs[slot_rows(e, e), :]

    def tangent_copy(zs, d):
        ref = tang.at[pl.ds(zs * CORES, CORES), mine]
        return remote(ref, ref, t_send.at[zs, d], t_recv.at[zs, e], (p, e_peer(d)))

    def rows_out(zs):
        two = pl.ds(pl.multiple_of(zs * CORES * rows, CORES * rows), CORES * rows)
        src = hall.reshape(n_dp * rows, hall.shape[2])
        return pltpu.make_async_copy(src.at[two], hall_out.at[two], out_sem.at[0, zs])

    def tangents(zs):
        rows_out(zs).start()
        block = hall[pl.ds(zs * CORES, CORES)].reshape(CORES * rows, hall.shape[2])
        out = jnp.dot(block, dirt[...], preferred_element_type=jnp.float32)
        tang[pl.ds(zs * CORES, CORES), mine, :feat] = out.astype(jnp.bfloat16).reshape(CORES, rows, feat)
        for d in range(1, n_e):
            tangent_copy(zs, d).start()

    load_dir.wait()
    dirt[...] = dirv[...].T
    load_h.wait()
    sibling_copy(z, h_ref).wait_recv()
    tangents(z)

    def weight_copy(side):
        to = z + 1 if side == 0 else z - 1
        return remote(wall.at[p], wall.at[p], w_send.at[side], w_recv.at[z], (to * CORES + core, e))

    def weight_relay(zs):
        to = jnp.where(zs < z, z + 1, z - 1)
        ref = wall.at[zs * CORES + core]
        return remote(ref, ref, wr_send.at[zs], w_recv.at[zs], (to * CORES + core, e))

    def weight_sibling(zs):
        ref = wall.at[zs * CORES + core]
        return remote(ref, ref, ws_send.at[zs], ws_recv.at[zs], (sib, e))

    def share_weights():
        for d in range(1, n_e):
            src = e_peer(d)
            remote(
                pairs.at[slot_rows(e, src)], wf.at[pl.ds(pl.multiple_of(src * cap, cap), cap)],
                a_send.at[d], a_recv.at[src], (p, src),
            ).wait_recv()
        weights = wf[...]
        high = weights.astype(jnp.bfloat16).astype(jnp.float32)
        wall[p] = (high + swap_blocks(weights - high, cap)).astype(jnp.bfloat16)
        for side in range(2):
            on_side(side, lambda side=side: weight_copy(side).start())
        weight_sibling(z).start()

    def forward_weights(zs):
        weight_relay(zs).wait_recv()
        relays(zs, lambda: weight_relay(zs).start())
        weight_sibling(zs).start()

    near = jnp.minimum(z, n_z - 1 - z)

    def source(j):
        if j == 0:
            return z
        s = (j + 1) // 2
        close = z + s if j % 2 else z - s
        far = jnp.where(2 * z < n_z - 1, j, n_z - 1 - j)
        return jnp.where(j <= 2 * near, close, far)

    def relay_copy(zs, c):
        to = jnp.where(zs < z, z + 1, z - 1)
        ref = hall.at[zs * CORES + core, pl.ds(c * part, part)]
        return remote(ref, ref, relay_send.at[zs, c], hz_recv.at[zs, c], (to * CORES + core, e))

    def relays(zs, fn):
        to = jnp.where(zs < z, z + 1, z - 1)
        pl.when((to >= 0) & (to < n_z))(fn)

    lane = lax.broadcasted_iota(jnp.int32, (rows, LANES), 1)
    row = lax.broadcasted_iota(jnp.int32, (rows, LANES), 0)
    direct = (lane // cap) % n_e == row // cap

    def adjoint_out(zs):
        two = pl.ds(pl.multiple_of(zs * CORES * rows, CORES * rows), CORES * rows)
        return pltpu.make_async_copy(adj.at[two], adj_out.at[two], out_sem.at[1, zs])

    def finish(zs):
        weight_sibling(zs).wait_recv()
        for d in range(1, n_e):
            src = e_peer(d)
            ref = tang.at[pl.ds(zs * CORES, CORES), pl.ds(pl.multiple_of(src * rows, rows), rows)]
            remote(ref, ref, t_send.at[zs, d], t_recv.at[zs, src], (p, src)).wait_recv()
        for k in range(CORES):
            packed = wall[zs * CORES + k].astype(jnp.float32)
            high = jnp.where(direct, packed, 0.0)
            low = swap_blocks(packed - high, cap)
            both = jnp.concatenate([high, low], axis=0).astype(jnp.bfloat16)
            out = jnp.dot(both, tang[zs * CORES + k], preferred_element_type=jnp.float32)
            out = (out[:rows] + out[rows:]).astype(jnp.bfloat16)
            adj[pl.ds(pl.multiple_of((zs * CORES + k) * rows, rows), rows), :] = out[:, :feat]
        adjoint_out(zs).start()

    def take(zs):
        for c in range(CHUNKS):
            relay_copy(zs, c).wait_recv()
            relays(zs, lambda c=c: relay_copy(zs, c).start())
        sibling_copy(zs, hall.at[zs * CORES + core]).start()

    for j in range(1, n_z):
        zs = source(j)
        if j == 2:
            pl.when(near == 0)(lambda zs=zs: take(zs))
        else:
            take(zs)
        if j == 1:
            pl.when(near > 0)(lambda: take(source(2)))
            share_weights()
        if j >= 2:
            forward_weights(source(j - 1))
            finish(source(j - 2))
        sibling_copy(zs, hall.at[zs * CORES + core]).wait_recv()
        tangents(zs)
    forward_weights(source(n_z - 1))
    finish(source(n_z - 2))
    finish(source(n_z - 1))

    for c in range(CHUNKS):
        for side in range(2):
            on_side(side, lambda side=side, c=c: own_copy(side, c).wait_send())
    for d in range(1, n_e):
        pair_copy(d).wait_send()
    for side in range(2):
        on_side(side, lambda side=side: weight_copy(side).wait_send())
    for j in range(n_z):
        zs = source(j)
        adjoint_out(zs).wait()
        rows_out(zs).wait()
        sibling_copy(zs, hall.at[zs * CORES + core]).wait_send()
        weight_sibling(zs).wait_send()
        for d in range(1, n_e):
            tangent_copy(zs, d).wait_send()
        if j:
            for c in range(CHUNKS):
                relays(zs, lambda zs=zs, c=c: relay_copy(zs, c).wait_send())
            relays(zs, lambda zs=zs: weight_relay(zs).wait_send())


def body(cached_hidden, direction, expert_ids, gate_weights):
    n_dp, n_e = lax.axis_size("dp"), lax.axis_size("expert")
    rows, fw = cached_hidden.shape
    cap = rows // n_e
    feat = direction.shape[1]
    if n_e * rows != LANES or cap % 8 or rows % (16 * CHUNKS) or n_dp % CORES or n_dp < 2 * CORES:
        return general_body(cached_hidden, direction, expert_ids, gate_weights)
    n_z = n_dp // CORES
    wide = -(-feat // LANES) * LANES
    scale = 1.0 / math.sqrt(expert_ids.shape[0] * n_dp * n_e)
    hbm = pl.BlockSpec(memory_space=pltpu.HBM)
    dma = pltpu.SemaphoreType.DMA
    adjoint, rows_all = pl.pallas_call(
        functools.partial(kernel, n_dp, n_e, cap, scale),
        out_shape=(
            jax.ShapeDtypeStruct((n_dp * rows, feat), jnp.bfloat16),
            jax.ShapeDtypeStruct((n_dp * rows, fw), jnp.bfloat16),
        ),
        in_specs=[hbm] * 4,
        out_specs=(hbm, hbm),
        scratch_shapes=[
            pltpu.VMEM((n_dp * rows, feat), jnp.bfloat16),
            pltpu.VMEM((n_dp, rows, fw), jnp.bfloat16),
            pltpu.VMEM((feat, fw), jnp.bfloat16),
            pltpu.VMEM((fw, feat), jnp.bfloat16),
            pltpu.VMEM(expert_ids.shape[::-1], jnp.int32),
            pltpu.VMEM(gate_weights.shape[::-1], jnp.float32),
            pltpu.VMEM((n_dp, n_e * rows, wide), jnp.bfloat16),
            pltpu.VMEM((LANES, LANES), jnp.float32),
            pltpu.VMEM((rows, LANES), jnp.float32),
            pltpu.VMEM((n_dp, rows, LANES), jnp.bfloat16),
            dma((4,)),
            dma((2, n_z)),
            dma((2, CHUNKS)),
            dma((n_z, CHUNKS)),
            dma((n_z, CHUNKS)),
            dma((n_z,)),
            dma((n_z,)),
            dma((n_e,)),
            dma((n_e,)),
            dma((2,)),
            dma((n_z,)),
            dma((n_z,)),
            dma((n_z,)),
            dma((n_z,)),
            dma((n_z, n_e)),
            dma((n_z, n_e)),
        ],
        compiler_params=pltpu.CompilerParams(
            collective_id=0, has_side_effects=True, vmem_limit_bytes=56 * 1024 * 1024
        ),
    )(cached_hidden, direction, expert_ids.T, gate_weights.T)
    gradient = lax.dot_general(
        adjoint,
        rows_all,
        (((0,), (0,)), ((), ())),
        preferred_element_type=jnp.float32,
    )
    return gradient.reshape(1, feat, fw)


def solution(mesh):
    return jax.shard_map(
        body,
        mesh=mesh,
        in_specs=(
            P(("dp", "expert"), None),
            P("expert", "dp", None),
            P(("dp", "expert"), None),
            P(("dp", "expert"), None),
        ),
        out_specs=P("expert", "dp", None),
        check_vma=False,
    )
```

```python
import functools
import math

import jax
import jax.numpy as jnp
from jax import lax
from jax.experimental import pallas as pl
from jax.experimental.pallas import tpu as pltpu
from jax.sharding import PartitionSpec as P

MESH = pl.DeviceIdType.MESH
CORES = 2
LANES = 128
CHUNKS = 2


def slot_positions(block_ids, experts):
    flat = block_ids.reshape(-1)
    onehot = (flat[:, None] == jnp.arange(experts, dtype=jnp.int32)[None, :]).astype(jnp.int32)
    before = jnp.cumsum(onehot, axis=0) - onehot
    return jnp.sum(before * onehot, axis=1).reshape(block_ids.shape)


def general_body(cached_hidden, direction, expert_ids, gate_weights):
    dp_count = lax.axis_size("dp")
    owner_count = lax.axis_size("expert")
    slot_rows = cached_hidden.shape[0]
    capacity = slot_rows // owner_count
    tok_count = expert_ids.shape[0]
    width = direction.shape[1] * dp_count
    local_dir = direction[0]
    rows_all = lax.all_gather(cached_hidden, "dp", axis=0, tiled=True)
    tangent = lax.dot_general(
        rows_all, local_dir, (((1,), (1,)), ((), ())), preferred_element_type=jnp.float32
    )
    tangent = tangent.astype(jnp.bfloat16).reshape(
        dp_count, owner_count, capacity, local_dir.shape[0]
    )
    returned = lax.all_to_all(
        lax.all_to_all(tangent, "dp", split_axis=0, concat_axis=3, tiled=True),
        "expert",
        split_axis=1,
        concat_axis=1,
        tiled=True,
    )
    flat_rows = returned.reshape(owner_count * capacity, width)
    treated = expert_ids < owner_count
    slot_pos = slot_positions(expert_ids, owner_count)
    target = expert_ids * capacity + slot_pos
    lookup = jnp.where(treated, target, 0).reshape(-1)
    dropped = jnp.where(treated, target, owner_count * capacity).reshape(-1)
    gates = jnp.where(treated, gate_weights, 0.0)
    picked = jnp.take(flat_rows, lookup, axis=0).reshape(tok_count, expert_ids.shape[1], width)
    scale_factor = 1.0 / math.sqrt(tok_count * dp_count * owner_count)
    combined = jnp.sum(gates[..., None] * picked.astype(jnp.float32), axis=1) * scale_factor
    outgoing = (gates[..., None] * combined[:, None, :]).astype(jnp.bfloat16)
    buffer = jnp.zeros((owner_count * capacity, width), jnp.bfloat16)
    buffer = buffer.at[dropped].set(outgoing.reshape(-1, width), mode="drop")
    buffer = buffer.reshape(1, owner_count, capacity, width)
    arrived = lax.all_to_all(buffer, "expert", split_axis=1, concat_axis=1, tiled=True)
    adjoint = lax.all_to_all(arrived, "dp", split_axis=3, concat_axis=0, tiled=True)
    adjoint_rows = adjoint.reshape(-1, adjoint.shape[3])
    gradient = lax.dot_general(
        adjoint_rows, rows_all, (((0,), (0,)), ((), ())), preferred_element_type=jnp.float32
    )
    return gradient.reshape(1, gradient.shape[0], gradient.shape[1])


def swap_blocks(x, cap):
    lane = lax.broadcasted_iota(jnp.int32, x.shape, 1)
    back = pltpu.roll(x, LANES - cap, 1)
    ahead = pltpu.roll(x, cap, 1)
    return jnp.where((lane // cap) % 2 == 0, back, ahead)


def pair_matrix(ids, gates, q, n_e, cap, scale):
    topk, toks = ids.shape
    slot = lax.broadcasted_iota(jnp.int32, (LANES, toks), 0)
    slot_e, slot_q, slot_c = slot // (n_e * cap), (slot // cap) % n_e, slot % cap
    named = jnp.zeros((LANES, toks), jnp.float32)
    gate = jnp.zeros((LANES, toks), jnp.float32)
    for k in range(topk):
        same = ids[k : k + 1, :] == slot_e
        named = named + jnp.where(same, 1.0, 0.0)
        gate = gate + jnp.where(same, gates[k : k + 1, :], 0.0)
    row = lax.broadcasted_iota(jnp.int32, (toks, toks), 0)
    col = lax.broadcasted_iota(jnp.int32, (toks, toks), 1)
    earlier = jnp.where(row < col, 1.0, 0.0).astype(jnp.bfloat16)
    position = jnp.dot(named.astype(jnp.bfloat16), earlier, preferred_element_type=jnp.float32)
    held = (position == slot_c.astype(jnp.float32)) & (slot_q == q)
    slots = jnp.where(held, gate, 0.0)
    high = slots.astype(jnp.bfloat16)
    low = (slots - high.astype(jnp.float32)).astype(jnp.bfloat16)
    nt = (((1,), (1,)), ((), ()))
    total = lax.dot_general(high, high, nt, preferred_element_type=jnp.float32)
    total += lax.dot_general(high, low, nt, preferred_element_type=jnp.float32)
    total += lax.dot_general(low, high, nt, preferred_element_type=jnp.float32)
    return total * scale


def kernel(
    n_dp, n_e, cap, scale,
    h_ref, dir_ref, ids_ref, gates_ref,
    adj_out, hall_out,
    adj, hall, dirv, dirt, idv, gatev, tang, pairs, wf, wall,
    loc_sem, out_sem, own_send, relay_send, hz_recv, hs_send, hs_recv,
    a_send, a_recv, w_send, wr_send, w_recv, ws_send, ws_recv, t_send, t_recv,
):
    n_z = n_dp // CORES
    rows = n_e * cap
    feat = dirv.shape[0]
    part = rows // CHUNKS
    p = lax.axis_index("dp")
    e = lax.axis_index("expert")
    z, core = p // CORES, p % CORES
    sib = z * CORES + (1 - core)

    load_dir = pltpu.make_async_copy(dir_ref.at[0], dirv, loc_sem.at[0])
    load_h = pltpu.make_async_copy(h_ref, hall.at[p], loc_sem.at[1])
    load_ids = pltpu.make_async_copy(ids_ref, idv, loc_sem.at[2])
    load_gates = pltpu.make_async_copy(gates_ref, gatev, loc_sem.at[3])
    load_ids.start()
    load_gates.start()
    load_h.start()
    load_dir.start()

    def on_side(side, fn):
        pl.when(z + 1 < n_z if side == 0 else z > 0)(fn)

    def e_peer(d):
        return lax.rem(e + d, n_e)

    barrier = pltpu.get_barrier_semaphore()
    for side in range(2):
        to = (z + 1 if side == 0 else z - 1) * CORES + core
        on_side(
            side,
            lambda to=to: pl.semaphore_signal(barrier, inc=1, device_id=(to, e), device_id_type=MESH),
        )
    for d in range(1, n_e):
        pl.semaphore_signal(barrier, inc=1, device_id=(p, e_peer(d)), device_id_type=MESH)
    pl.semaphore_signal(barrier, inc=1, device_id=(sib, e), device_id_type=MESH)
    mine = pl.ds(pl.multiple_of(e * rows, rows), rows)
    tang[:, mine, feat // LANES * LANES :] = jnp.zeros(
        (n_dp, rows, tang.shape[2] - feat // LANES * LANES), jnp.bfloat16
    )
    on_line = jnp.where(z > 0, 1, 0) + jnp.where(z + 1 < n_z, 1, 0)
    pl.semaphore_wait(barrier, on_line + n_e)

    def remote(src, dst, send, recv, dev):
        return pltpu.make_async_remote_copy(
            src_ref=src, dst_ref=dst, send_sem=send, recv_sem=recv, device_id=dev, device_id_type=MESH
        )

    def own_copy(side, c):
        to = z + 1 if side == 0 else z - 1
        return remote(
            h_ref.at[pl.ds(c * part, part)], hall.at[p, pl.ds(c * part, part)],
            own_send.at[side, c], hz_recv.at[z, c], (to * CORES + core, e),
        )

    for c in range(CHUNKS):
        for side in (1, 0):
            on_side(side, lambda side=side, c=c: own_copy(side, c).start())

    def sibling_copy(zs, src):
        row = zs * CORES + core
        return remote(src, hall.at[row], hs_send.at[zs], hs_recv.at[zs], (sib, e))

    sibling_copy(z, h_ref).start()

    load_ids.wait()
    load_gates.wait()
    pairs[...] = pair_matrix(idv[...], gatev[...], e, n_e, cap, scale)

    def slot_rows(owner, source):
        return pl.ds(pl.multiple_of(owner * rows + source * cap, cap), cap)

    def pair_copy(d):
        to = e_peer(d)
        return remote(
            pairs.at[slot_rows(to, e)], wf.at[pl.ds(pl.multiple_of(e * cap, cap), cap)],
            a_send.at[d], a_recv.at[e], (p, to),
        )

    for d in range(1, n_e):
        pair_copy(d).start()
    wf[pl.ds(pl.multiple_of(e * cap, cap), cap), :] = pairs[slot_rows(e, e), :]

    def tangent_copy(zs, d):
        ref = tang.at[pl.ds(zs * CORES, CORES), mine]
        return remote(ref, ref, t_send.at[zs, d], t_recv.at[zs, e], (p, e_peer(d)))

    def rows_out(zs):
        two = pl.ds(pl.multiple_of(zs * CORES * rows, CORES * rows), CORES * rows)
        src = hall.reshape(n_dp * rows, hall.shape[2])
        return pltpu.make_async_copy(src.at[two], hall_out.at[two], out_sem.at[0, zs])

    def tangents(zs):
        rows_out(zs).start()
        block = hall[pl.ds(zs * CORES, CORES)].reshape(CORES * rows, hall.shape[2])
        out = jnp.dot(block, dirt[...], preferred_element_type=jnp.float32)
        tang[pl.ds(zs * CORES, CORES), mine, :feat] = out.astype(jnp.bfloat16).reshape(CORES, rows, feat)
        for d in range(1, n_e):
            tangent_copy(zs, d).start()

    load_dir.wait()
    dirt[...] = dirv[...].T
    load_h.wait()
    sibling_copy(z, h_ref).wait_recv()
    tangents(z)

    def weight_copy(side):
        to = z + 1 if side == 0 else z - 1
        return remote(wall.at[p], wall.at[p], w_send.at[side], w_recv.at[z], (to * CORES + core, e))

    def weight_relay(zs):
        to = jnp.where(zs < z, z + 1, z - 1)
        ref = wall.at[zs * CORES + core]
        return remote(ref, ref, wr_send.at[zs], w_recv.at[zs], (to * CORES + core, e))

    def weight_sibling(zs):
        ref = wall.at[zs * CORES + core]
        return remote(ref, ref, ws_send.at[zs], ws_recv.at[zs], (sib, e))

    def share_weights():
        for d in range(1, n_e):
            src = e_peer(d)
            remote(
                pairs.at[slot_rows(e, src)], wf.at[pl.ds(pl.multiple_of(src * cap, cap), cap)],
                a_send.at[d], a_recv.at[src], (p, src),
            ).wait_recv()
        weights = wf[...]
        high = weights.astype(jnp.bfloat16).astype(jnp.float32)
        wall[p] = (high + swap_blocks(weights - high, cap)).astype(jnp.bfloat16)
        for side in range(2):
            on_side(side, lambda side=side: weight_copy(side).start())
        weight_sibling(z).start()

    def forward_weights(zs):
        weight_relay(zs).wait_recv()
        relays(zs, lambda: weight_relay(zs).start())
        weight_sibling(zs).start()

    near = jnp.minimum(z, n_z - 1 - z)

    def source(j):
        if j == 0:
            return z
        s = (j + 1) // 2
        close = z + s if j % 2 else z - s
        far = jnp.where(2 * z < n_z - 1, j, n_z - 1 - j)
        return jnp.where(j <= 2 * near, close, far)

    def relay_copy(zs, c):
        to = jnp.where(zs < z, z + 1, z - 1)
        ref = hall.at[zs * CORES + core, pl.ds(c * part, part)]
        return remote(ref, ref, relay_send.at[zs, c], hz_recv.at[zs, c], (to * CORES + core, e))

    def relays(zs, fn):
        to = jnp.where(zs < z, z + 1, z - 1)
        pl.when((to >= 0) & (to < n_z))(fn)

    lane = lax.broadcasted_iota(jnp.int32, (rows, LANES), 1)
    row = lax.broadcasted_iota(jnp.int32, (rows, LANES), 0)
    direct = (lane // cap) % n_e == row // cap

    def adjoint_out(zs):
        two = pl.ds(pl.multiple_of(zs * CORES * rows, CORES * rows), CORES * rows)
        return pltpu.make_async_copy(adj.at[two], adj_out.at[two], out_sem.at[1, zs])

    def finish(zs):
        weight_sibling(zs).wait_recv()
        for d in range(1, n_e):
            src = e_peer(d)
            ref = tang.at[pl.ds(zs * CORES, CORES), pl.ds(pl.multiple_of(src * rows, rows), rows)]
            remote(ref, ref, t_send.at[zs, d], t_recv.at[zs, src], (p, src)).wait_recv()
        for k in range(CORES):
            packed = wall[zs * CORES + k].astype(jnp.float32)
            high = jnp.where(direct, packed, 0.0)
            low = swap_blocks(packed - high, cap)
            both = jnp.concatenate([high, low], axis=0).astype(jnp.bfloat16)
            out = jnp.dot(both, tang[zs * CORES + k], preferred_element_type=jnp.float32)
            out = (out[:rows] + out[rows:]).astype(jnp.bfloat16)
            adj[pl.ds(pl.multiple_of((zs * CORES + k) * rows, rows), rows), :] = out[:, :feat]
        adjoint_out(zs).start()

    def take(zs):
        for c in range(CHUNKS):
            relay_copy(zs, c).wait_recv()
            relays(zs, lambda c=c: relay_copy(zs, c).start())
        sibling_copy(zs, hall.at[zs * CORES + core]).start()

    for j in range(1, n_z):
        zs = source(j)
        if j in (2, 3):
            pl.when(near == 0)(lambda zs=zs: take(zs))
            if j == 2 and n_z > 3:
                pl.when(near > 0)(lambda: take(source(3)))
        else:
            take(zs)
        if j == 1:
            pl.when(near > 0)(lambda: take(source(2)))
            share_weights()
        if j >= 2:
            forward_weights(source(j - 1))
            finish(source(j - 2))
        sibling_copy(zs, hall.at[zs * CORES + core]).wait_recv()
        tangents(zs)
    forward_weights(source(n_z - 1))
    finish(source(n_z - 2))
    finish(source(n_z - 1))

    for c in range(CHUNKS):
        for side in range(2):
            on_side(side, lambda side=side, c=c: own_copy(side, c).wait_send())
    for d in range(1, n_e):
        pair_copy(d).wait_send()
    for side in range(2):
        on_side(side, lambda side=side: weight_copy(side).wait_send())
    for j in range(n_z):
        zs = source(j)
        adjoint_out(zs).wait()
        rows_out(zs).wait()
        sibling_copy(zs, hall.at[zs * CORES + core]).wait_send()
        weight_sibling(zs).wait_send()
        for d in range(1, n_e):
            tangent_copy(zs, d).wait_send()
        if j:
            for c in range(CHUNKS):
                relays(zs, lambda zs=zs, c=c: relay_copy(zs, c).wait_send())
            relays(zs, lambda zs=zs: weight_relay(zs).wait_send())


def body(cached_hidden, direction, expert_ids, gate_weights):
    n_dp, n_e = lax.axis_size("dp"), lax.axis_size("expert")
    rows, fw = cached_hidden.shape
    cap = rows // n_e
    feat = direction.shape[1]
    if n_e * rows != LANES or cap % 8 or rows % (16 * CHUNKS) or n_dp % CORES or n_dp < 2 * CORES:
        return general_body(cached_hidden, direction, expert_ids, gate_weights)
    n_z = n_dp // CORES
    wide = -(-feat // LANES) * LANES
    scale = 1.0 / math.sqrt(expert_ids.shape[0] * n_dp * n_e)
    hbm = pl.BlockSpec(memory_space=pltpu.HBM)
    dma = pltpu.SemaphoreType.DMA
    adjoint, rows_all = pl.pallas_call(
        functools.partial(kernel, n_dp, n_e, cap, scale),
        out_shape=(
            jax.ShapeDtypeStruct((n_dp * rows, feat), jnp.bfloat16),
            jax.ShapeDtypeStruct((n_dp * rows, fw), jnp.bfloat16),
        ),
        in_specs=[hbm] * 4,
        out_specs=(hbm, hbm),
        scratch_shapes=[
            pltpu.VMEM((n_dp * rows, feat), jnp.bfloat16),
            pltpu.VMEM((n_dp, rows, fw), jnp.bfloat16),
            pltpu.VMEM((feat, fw), jnp.bfloat16),
            pltpu.VMEM((fw, feat), jnp.bfloat16),
            pltpu.VMEM(expert_ids.shape[::-1], jnp.int32),
            pltpu.VMEM(gate_weights.shape[::-1], jnp.float32),
            pltpu.VMEM((n_dp, n_e * rows, wide), jnp.bfloat16),
            pltpu.VMEM((LANES, LANES), jnp.float32),
            pltpu.VMEM((rows, LANES), jnp.float32),
            pltpu.VMEM((n_dp, rows, LANES), jnp.bfloat16),
            dma((4,)),
            dma((2, n_z)),
            dma((2, CHUNKS)),
            dma((n_z, CHUNKS)),
            dma((n_z, CHUNKS)),
            dma((n_z,)),
            dma((n_z,)),
            dma((n_e,)),
            dma((n_e,)),
            dma((2,)),
            dma((n_z,)),
            dma((n_z,)),
            dma((n_z,)),
            dma((n_z,)),
            dma((n_z, n_e)),
            dma((n_z, n_e)),
        ],
        compiler_params=pltpu.CompilerParams(
            collective_id=0, has_side_effects=True, vmem_limit_bytes=56 * 1024 * 1024
        ),
    )(cached_hidden, direction, expert_ids.T, gate_weights.T)
    gradient = lax.dot_general(
        adjoint,
        rows_all,
        (((0,), (0,)), ((), ())),
        preferred_element_type=jnp.float32,
    )
    return gradient.reshape(1, feat, fw)


def solution(mesh):
    return jax.shard_map(
        body,
        mesh=mesh,
        in_specs=(
            P(("dp", "expert"), None),
            P("expert", "dp", None),
            P(("dp", "expert"), None),
            P(("dp", "expert"), None),
        ),
        out_specs=P("expert", "dp", None),
        check_vma=False,
    )
```
